512 devices in a mesh: frames: 128 (over y, x, z_hi, core), rows: 4 (over z_lo).
Axes of the slice: x: 4, y: 4, z: 16 (z_hi: 4, z_lo: 4; z = z_hi * 4 + z_lo), core: 2. Of those that a mesh axis runs over, the one named last changes fastest.
Arguments:
- act: bfloat16 [384, 256, 4, 128], P(None, 'frames', 'rows'), may hold values from -600 to 600, as said below
- cotangent: bfloat16 [96, 256, 4, 128], P(None, 'frames', 'rows'), may hold values from -6 to 6
- kernel: bfloat16 [27, 96, 384], replicated, may hold values from -0.0625 to 0.0625
- gamma: float32 [384], replicated, may hold values from 0.5 to 1.5
- beta: float32 [384], replicated, may hold values from -3 to 3
Outputs:
- act_grad: bfloat16 [384, 256, 4, 128], P(None, 'frames', 'rows')
- kernel_grad: float32 [27, 36864], P(None, ('frames', 'rows'))
- gamma_grad: float32 [384], replicated
- beta_grad: float32 [384], replicated
- group_mean: float32 [16, 32], replicated
- group_rstd: float32 [16, 32], replicated
The draws below stay inside these ranges and needn't reach their ends.
Inputs may be any that keep to these rules, and one draw needn't show every extreme that they name: act has channel-dependent scales and offsets.
All inputs are finite; a program needn't handle non-finite values.
Results may differ from the reference program's by a relative error of at most 0.003.
Values may be sent and summed in bfloat16 or wider, within the bound.
A program may use at most 128 MiB of HBM per device.

```python
import jax
import jax.numpy as jnp
from jax import lax

C_IN = 384
C_OUT = 96
GROUPS = 32
KERNEL = 3
CLIP_FRAMES = 16
WIDTH = 128
FRAMES = 256
HEIGHT = 4


def draw_act(key, part):
    key = jax.random.fold_in(key, 7)
    keys = jax.random.split(key, 4)
    full_shape = (C_IN, FRAMES, HEIGHT, WIDTH)
    clip_place = (jnp.arange(FRAMES) % CLIP_FRAMES).astype(jnp.float32)
    along_t = (clip_place / max(CLIP_FRAMES - 1, 1)).reshape(1, FRAMES, 1, 1)
    along_h = (jnp.arange(HEIGHT, dtype=jnp.float32) / max(HEIGHT - 1, 1)).reshape(1, 1, HEIGHT, 1)
    rising = jnp.exp(jnp.log(3.0) * (along_t + along_h))
    rough = jax.random.uniform(keys[0], full_shape, jnp.float32, 0.5, 1.5)
    noise = jnp.clip(jax.random.normal(keys[1], full_shape, jnp.float32), -4.0, 4.0)
    spread = jnp.exp(jax.random.uniform(keys[2], (C_IN, 1, 1, 1), jnp.float32, 0.0, jnp.log(4.0)))
    offset = jax.random.uniform(keys[3], (C_IN, 1, 1, 1), jnp.float32, -1.0, 1.0)
    return (rising * (spread * noise * rough + offset * (along_t + along_h))).astype(jnp.bfloat16)


def shard_levels(own_key, shape, cuts, low, high):
    level, own = 1.0, jax.random.fold_in(own_key, 6)
    for dim, shards_of in cuts:
        heights = jnp.exp(jax.random.uniform(jax.random.fold_in(own, dim), (shards_of,), jnp.float32, low / len(cuts), high / len(cuts)))
        level = level * jnp.repeat(heights, shape[dim] // shards_of).reshape([-1 if axis == dim else 1 for axis in range(len(shape))])
    return level


def scatter_about(own_key, dims, deviation, reach, cuts=(), kind=jnp.bfloat16):
    array = jax.random.normal(own_key, dims, jnp.float32) * deviation
    if len(cuts) > 0:
        array = shard_levels(own_key, dims, cuts, -0.22, 0.18) * array
    return jnp.clip(array, min=-reach, max=reach).astype(kind)


def setup_inputs(seed: int = 0) -> dict:
    key_list = jax.random.split(jax.random.key(seed), 6)
    act = draw_act(jax.random.fold_in(key_list[5], 71), 0)
    cotangent = scatter_about(key_list[1], (C_OUT, FRAMES, HEIGHT, WIDTH), 1.0, 6.0, ((1, 128), (2, 4)))
    kernel = scatter_about(key_list[2], (KERNEL**3, C_OUT, C_IN), (KERNEL**3 * C_IN) ** -0.5, 0.0625)
    gamma = jnp.clip(jax.random.uniform(key_list[3], (C_IN,), jnp.float32, 0.5, 1.5), 0.5, 1.5)
    beta = scatter_about(key_list[4], (C_IN,), 1.0, 3.0, (), jnp.float32)
    return dict(act=act, cotangent=cotangent, kernel=kernel, gamma=gamma, beta=beta)


EPS = 1e-06

def reference(act, cotangent, kernel, gamma, beta):
    causal_lead = KERNEL - 1
    margin = (KERNEL - 1) // 2
    clip_count = FRAMES // CLIP_FRAMES
    per_group = C_IN // GROUPS
    cells_clip = CLIP_FRAMES * HEIGHT * WIDTH
    cells_all = FRAMES * HEIGHT * WIDTH
    group_count = per_group * cells_clip
    grouped = act.astype(jnp.float32).reshape(GROUPS, per_group, clip_count, cells_clip)
    mean_gc = lax.optimization_barrier(jnp.sum(grouped, axis=(1, 3))) / group_count
    centred = grouped - mean_gc[:, None, :, None]
    variance = lax.optimization_barrier(jnp.sum(centred * centred, axis=(1, 3))) / group_count
    rstd_gc = lax.rsqrt(variance + EPS)
    normed = (centred * rstd_gc[:, None, :, None]).reshape(act.shape)
    shaped = normed * gamma[:, None, None, None] + beta[:, None, None, None]
    hidden = jax.nn.silu(shaped).astype(jnp.bfloat16)
    hidden_clip = hidden.reshape(C_IN, clip_count, CLIP_FRAMES, HEIGHT, WIDTH)
    grad_clip = cotangent.reshape(C_OUT, clip_count, CLIP_FRAMES, HEIGHT, WIDTH)
    padded_act = jnp.pad(hidden_clip, ((0, 0), (0, 0), (causal_lead, 0), (margin, margin), (margin, margin)))
    padded_grad = jnp.pad(grad_clip, ((0, 0), (0, 0), (0, causal_lead), (margin, margin), (margin, margin)))
    flat_grad = cotangent.reshape(C_OUT, -1)
    hidden_grad = jnp.zeros((C_IN, cells_all), jnp.float32)
    kernel_rows = []
    for step_t in range(KERNEL):
        for step_h in range(KERNEL):
            for step_w in range(KERNEL):
                tap_index = step_t * KERNEL * KERNEL + step_h * KERNEL + step_w
                window = padded_act[:, :, step_t:step_t + CLIP_FRAMES, step_h:step_h + HEIGHT, step_w:step_w + WIDTH].reshape(C_IN, -1)
                kernel_rows.append(lax.dot_general(window, flat_grad, (((1,), (1,)), ((), ())), preferred_element_type=jnp.float32))
                source = padded_grad[:, :, causal_lead - step_t:causal_lead - step_t + CLIP_FRAMES, 2 * margin - step_h:2 * margin - step_h + HEIGHT, 2 * margin - step_w:2 * margin - step_w + WIDTH].reshape(C_OUT, -1)
                hidden_grad = hidden_grad + lax.dot_general(kernel[tap_index], source, (((0,), (0,)), ((), ())), preferred_element_type=jnp.float32)
    sigmoid_z = jax.nn.sigmoid(shaped)
    shaped_grad = hidden_grad.reshape(shaped.shape) * sigmoid_z * (1.0 + shaped * (1.0 - sigmoid_z))
    grad_cells = shaped_grad.reshape(C_IN, clip_count, cells_clip)
    normed_cells = normed.reshape(C_IN, clip_count, cells_clip)
    gamma_clip = lax.optimization_barrier(jnp.sum(grad_cells * normed_cells, axis=2))
    beta_clip = lax.optimization_barrier(jnp.sum(grad_cells, axis=2))
    first = lax.optimization_barrier(jnp.sum((gamma[:, None] * beta_clip).reshape(GROUPS, per_group, clip_count), axis=1)) / group_count
    second = lax.optimization_barrier(jnp.sum((gamma[:, None] * gamma_clip).reshape(GROUPS, per_group, clip_count), axis=1)) / group_count
    normed_grad = (grad_cells * gamma[:, None, None]).reshape(GROUPS, per_group, clip_count, cells_clip)
    normed_group = normed_cells.reshape(GROUPS, per_group, clip_count, cells_clip)
    act_grad = rstd_gc[:, None, :, None] * (normed_grad - first[:, None, :, None] - normed_group * second[:, None, :, None])
    act_grad = act_grad.reshape(act.shape).astype(jnp.bfloat16)
    scale = float(cells_all) ** (-0.5)
    kernel_grad = jnp.stack(kernel_rows).reshape(KERNEL ** 3, C_IN * C_OUT) * scale
    gamma_grad = lax.optimization_barrier(jnp.sum(gamma_clip, axis=1)) * scale
    beta_grad = lax.optimization_barrier(jnp.sum(beta_clip, axis=1)) * scale
    return (act_grad, kernel_grad, gamma_grad, beta_grad, mean_gc.T, rstd_gc.T)
```

```python
import functools

import jax
import jax.numpy as jnp
from jax import lax
from jax.experimental import pallas as pl
from jax.experimental.pallas import tpu as pltpu
from jax.sharding import PartitionSpec as P

GROUPS = 32
KERNEL = 3
LANES = 128
EPS = 1e-06
F32 = jnp.float32
BF16 = jnp.bfloat16
MESH = pl.DeviceIdType.MESH


def remote(src, dst, send_sem, recv_sem, device):
    return pltpu.make_async_remote_copy(
        src_ref=src,
        dst_ref=dst,
        send_sem=send_sem,
        recv_sem=recv_sem,
        device_id=device,
        device_id_type=MESH,
    )


def others(count, me, step, farthest=False):
    def body(d, carry):
        if farthest:
            d = count // 2 + (d // 2) * (1 - 2 * lax.rem(d, 2))
        step(lax.rem(me + d, count))
        return carry

    lax.fori_loop(1, count, body, 0)


def exchange(buf, send, recv, count, me, device):
    def copy(slot, peer):
        return remote(buf.at[slot], buf.at[slot], send.at[peer], recv.at[slot], device(peer))

    return (
        lambda: others(count, me, lambda p: copy(me, p).start(), True),
        lambda: others(count, me, lambda p: copy(p, p).wait_recv()),
        lambda: others(count, me, lambda p: copy(me, p).wait_send()),
    )


def listed(buf):
    return jnp.concatenate([buf[n] for n in range(buf.shape[0])], axis=0)


def body(
    sizes,
    act_ref,
    cot_ref,
    kernel_ref,
    gamma_ref,
    beta_ref,
    act_grad_ref,
    kernel_grad_ref,
    gamma_grad_ref,
    beta_grad_ref,
    mean_ref,
    rstd_ref,
    act_raw,
    cot_raw,
    gamma_raw,
    beta_raw,
    act_grad,
    kernel_grad,
    gamma_grad,
    beta_grad,
    mean_table,
    rstd_table,
    x_ref,
    stats,
    ring,
    groups,
    affine,
    affine_all,
    blocks,
    slabs,
    weights,
    perm,
    mask_a,
    mask_b,
    gain,
    own_mask,
    own_gain,
    normed_ref,
    slope_ref,
    grad_ref,
    act_out,
    act_in,
    partial,
    by_owner,
    plane_out,
    plane_in,
    column_out,
    column_in,
    load_sem,
    store_sem,
    stats_s,
    stats_r,
    ring_s,
    ring_r,
    groups_s,
    groups_r,
    affine_s,
    affine_r,
    all_s,
    all_r,
    line_s,
    mate_s,
    next_s,
    next_line_s,
    pass_s,
    blocks_r,
    act_s,
    act_r,
    plane_s,
    plane_r,
    column_s,
    column_r,
):
    Z, YX, C, O, group_count, scale = sizes
    per_group = C // GROUPS
    half = act_raw.shape[2]
    cells = 2 * half
    width = 3 * YX
    column = 2 * Z * Z
    padded = affine_all.shape[2] // 2
    f = lax.axis_index("frames")
    zl = lax.axis_index("rows")
    core = lax.rem(f, 2)
    zh = lax.rem(f // 2, Z)
    yx = f // (2 * Z)
    rank = lax.rem(f, 2 * Z) * Z + zl
    member = core * Z + zl

    def in_column(p):
        return (yx * (2 * Z) + p // Z, lax.rem(p, Z))

    def in_plane(p):
        return (p * (2 * Z) + lax.rem(f, 2 * Z), zl)

    def in_block(p):
        return (yx * (2 * Z) + zh * 2 + p // Z, lax.rem(p, Z))

    mate = (f + 1 - 2 * core, zl)

    def across_blocks(step):
        return (yx * (2 * Z) + lax.rem(zh + step + Z, Z) * 2 + core, zl)

    partner = (yx * (2 * Z) + lax.rem(zh + 2 * core - 1 + Z, Z) * 2 + 1 - core, zl)
    steps = [Z // 2] + [step for n in range(1, Z // 2) for step in (n, -n)]

    barrier = pltpu.get_barrier_semaphore()

    def greet(device):
        pl.semaphore_signal(barrier, inc=1, device_id=device, device_id_type=MESH)

    for step in steps:
        greet(across_blocks(step))
    greet(partner)
    others(YX, yx, lambda p: greet(in_plane(p)), True)
    others(2 * Z, member, lambda p: greet(in_block(p)))

    loads = [
        pltpu.make_async_copy(source, target, load_sem.at[n])
        for n, (source, target) in enumerate(
            (
                (act_ref, act_raw),
                (cot_ref, cot_raw),
                (gamma_ref, gamma_raw),
                (beta_ref, beta_raw),
                (kernel_ref, weights.at[:, pl.ds(0, O), :]),
            )
        )
    ]
    for load in loads:
        load.start()

    chan = lax.broadcasted_iota(jnp.int32, (C, LANES), 0)
    lane = lax.broadcasted_iota(jnp.int32, (C, LANES), 1)
    first_chan = lane * per_group
    mask_a[...] = jnp.where((chan >= first_chan) & (chan < first_chan + per_group), 1.0, 0.0).astype(F32)
    place = lax.broadcasted_iota(jnp.int32, (YX, C), 0) * (6 * Z)
    source = lax.broadcasted_iota(jnp.int32, (YX, C), 1)
    for p in range(2 * Z):
        for c in range(3):
            base = p * width + c * YX
            offset = (p % Z) * 6 + (p // Z) * 3 + c
            perm[base : base + YX, :] = jnp.where(source == place + offset, 1.0, 0.0).astype(BF16)

    loads[0].wait()
    x_a = act_raw[:, 0, :].astype(F32)
    x_b = act_raw[:, 1, :].astype(F32)
    x_ref[:, :half] = x_a
    x_ref[:, half:] = x_b
    mean = jnp.sum(x_a + x_b, axis=1, keepdims=True) / cells
    squares = jnp.sum((x_a - mean) * (x_a - mean) + (x_b - mean) * (x_b - mean), axis=1, keepdims=True)
    mean_row = jnp.sum(mask_a[...] * mean, axis=0, keepdims=True) / per_group
    gap = mean - jnp.sum(mask_a[...] * mean_row, axis=1, keepdims=True)
    squares = squares + cells * (gap * gap)
    stats[member] = mean_row + pltpu.roll(jnp.sum(mask_a[...] * squares, axis=0, keepdims=True), GROUPS, 1)

    loads[1].wait()
    for side in range(2):
        blocks[core, zl, :, side * half : (side + 1) * half] = cot_raw[:, side, :].astype(F32).astype(BF16)

    ordered = jnp.dot(perm[...], x_ref[...].astype(BF16), preferred_element_type=F32).astype(BF16)
    act_out[...] = ordered.reshape(act_out.shape)
    act_in[member] = act_out[member]

    pl.semaphore_wait(barrier, len(steps) + 1 + YX - 1 + 2 * Z - 1)

    def block_copy(pair, row, send, device):
        ref = blocks.at[pair, row]
        return remote(ref, ref, send, blocks_r.at[pair, row], device)

    side_rows = Z // 2
    own_half = zl // side_rows
    gateway = side_rows - own_half
    is_gateway = zl == side_rows - 1 + own_half

    def half_peers(step):
        others(side_rows, lax.rem(zl, side_rows), lambda n: step(own_half * side_rows + n))

    def to_line(pair, sems, act):
        half_peers(lambda p: act(block_copy(pair, zl, sems.at[p], (f, p))))
        act(block_copy(pair, zl, sems.at[gateway], (f, gateway)))

    def to_mate(pair, row, which):
        return block_copy(pair, row, mate_s.at[which, row], mate)

    def landed(pair, row):
        block_copy(pair, row, line_s.at[0], mate).wait_recv()

    def start(copy):
        copy.start()

    def wait_send(copy):
        copy.wait_send()

    def passed(pair, which, act):
        @pl.when(is_gateway)
        def _():
            def across(n, carry):
                row = (1 - own_half) * side_rows + n
                half_peers(lambda p: act(block_copy(pair, row, pass_s.at[which, row], (f, p))))
                return carry

            lax.fori_loop(0, side_rows, across, 0)

    def take_line(pair, which):
        def across(n, carry):
            row = (1 - own_half) * side_rows + n
            landed(pair, row)

            @pl.when(is_gateway)
            def _():
                half_peers(lambda p: block_copy(pair, row, pass_s.at[which, row], (f, p)).start())

            to_mate(pair, row, which).start()
            return carry

        def near():
            def step(p):
                landed(pair, p)
                to_mate(pair, p, which).start()

            half_peers(step)

        def far():
            lax.fori_loop(0, side_rows, across, 0)

        near()
        far()

    gives_next = (core == 0) & (zh > 0)
    takes_next = (core == 1) & (zh < Z - 1)
    earlier = (lax.max(f - 1, 0), zl)

    def block_copy_next():
        return remote(blocks.at[core, zl], blocks.at[2, zl], next_s.at[0], blocks_r.at[2, zl], earlier)

    @pl.when(gives_next)
    def _():
        block_copy_next().start()

    start_stats, recv_stats, sent_stats = exchange(stats, stats_s, stats_r, 2 * Z, member, in_block)
    start_stats()
    to_line(core, line_s, start)
    to_mate(core, zl, 0).start()

    def act_copy(peer, slot):
        return remote(act_out.at[peer], act_in.at[slot], act_s.at[peer], act_r.at[slot], in_block(peer))

    others(2 * Z, member, lambda p: act_copy(p, member).start())

    first_chan = (lane - GROUPS) * per_group
    mask_b[...] = jnp.where((chan >= first_chan) & (chan < first_chan + per_group), 1.0, 0.0).astype(F32)
    loads[2].wait()
    loads[3].wait()
    gamma_row = gamma_raw[...].reshape(1, C)
    beta_row = beta_raw[...].reshape(1, C)
    gain[0] = jnp.broadcast_to(gamma_row, (LANES, C)).T
    gain[1] = jnp.broadcast_to(beta_row, (LANES, C)).T
    own_chan = lax.broadcasted_iota(jnp.int32, (YX, LANES), 0) * (6 * Z)
    own_lane = lax.broadcasted_iota(jnp.int32, (YX, LANES), 1) * per_group
    for c in range(3):
        at = pl.ds(c * YX, YX)
        offset = zl * 6 + core * 3 + c
        chosen = jnp.where(source == place + offset, 1.0, 0.0).astype(F32)
        own_gain[0, at, :] = jnp.broadcast_to(jnp.sum(chosen * gamma_row, axis=1, keepdims=True), (YX, LANES))
        own_gain[1, at, :] = jnp.broadcast_to(jnp.sum(chosen * beta_row, axis=1, keepdims=True), (YX, LANES))
        inside = (own_chan + offset >= own_lane) & (own_chan + offset < own_lane + per_group)
        own_mask[at, :] = jnp.where(inside, 1.0, 0.0).astype(F32)

    if O < LANES:
        weights[:, O:, :] = jnp.zeros((KERNEL**3, LANES - O, C), BF16)

    @pl.when(zh == Z - 1)
    def _():
        blocks[2] = jnp.zeros(blocks.shape[1:], BF16)

    slabs[:, 0] = jnp.zeros((5,) + slabs.shape[2:], BF16)
    slabs[:, Z + 1] = jnp.zeros((5,) + slabs.shape[2:], BF16)
    if O < LANES:
        for k in range(KERNEL):
            slabs[:, 1 : Z + 1, k * LANES + O : (k + 1) * LANES, :] = jnp.zeros((5, Z, LANES - O, cells), BF16)

    lane_row = lax.broadcasted_iota(jnp.int32, (1, LANES), 1)

    def combined(rows, cells_of_one):
        total = jnp.sum(rows, axis=0, keepdims=True)
        mean_row = jnp.where(lane_row < GROUPS, total / rows.shape[0], 0.0)
        gaps = jnp.where(lane_row < GROUPS, rows - mean_row, 0.0)
        return mean_row, pltpu.roll(total, LANES - GROUPS, 1) + cells_of_one * jnp.sum(gaps * gaps, axis=0, keepdims=True)

    recv_stats()
    block_mean, block_squares = combined(listed(stats), per_group * cells)
    ring[zh] = block_mean + pltpu.roll(jnp.where(lane_row < GROUPS, block_squares, 0.0), GROUPS, 1)

    def ring_copy(slot, which, step):
        return remote(ring.at[slot], ring.at[slot], ring_s.at[which], ring_r.at[slot], across_blocks(step))

    def block_at(step):
        return lax.rem(zh + step + Z, Z)

    for which, step in enumerate(steps):
        ring_copy(zh, which, step).start()

    take_line(core, 0)

    @pl.when(takes_next)
    def _():
        landed(2, zl)
        others(Z, zl, lambda p: block_copy(2, zl, next_line_s.at[p], (f, p)).start())
        to_mate(2, zl, 1).start()

    def from_mate(row, carry):
        landed(1 - core, row)
        return carry

    lax.fori_loop(0, Z, from_mate, 0)

    column_lane = lax.broadcasted_iota(jnp.int32, (O, half), 1)

    def fill(frames):
        def fill_row(row, carry):
            for frame in frames:
                slab = blocks[frame // 2, row, :, (frame % 2) * half : (frame % 2 + 1) * half]
                wide = slab.astype(F32)
                shifted = (
                    jnp.where(column_lane < half - 1, pltpu.roll(wide, half - 1, 1), 0.0).astype(BF16),
                    slab,
                    jnp.where(column_lane > 0, pltpu.roll(wide, 1, 1), 0.0).astype(BF16),
                )
                for k in range(KERNEL):
                    if frame < 5:
                        slabs[frame, row + 1, k * LANES : k * LANES + O, :half] = shifted[k]
                    if frame > 0:
                        slabs[frame - 1, row + 1, k * LANES : k * LANES + O, half:] = shifted[k]
            return carry

        lax.fori_loop(0, Z, fill_row, 0)

    fill(range(4))

    def gradient(lags):
        total = grad_ref[...]
        for i in lags:
            for j in range(KERNEL):
                tap = (i * KERNEL + j) * KERNEL
                total += lax.dot_general(
                    weights[tap : tap + KERNEL].reshape(KERNEL * LANES, C),
                    slabs[2 * core + 2 - i, zl - j + 2],
                    (((0,), (0,)), ((), ())),
                    preferred_element_type=F32,
                )
        grad_ref[...] = total

    loads[4].wait()
    grad_ref[...] = jnp.zeros((C, cells), F32)
    gradient((2,))


    for step in steps:
        ring_copy(block_at(step), 0, step).wait_recv()
    mean_row, squares_row = combined(listed(ring), 2 * Z * per_group * cells)
    rstd_row = jnp.where(
        lane_row < GROUPS, lax.rsqrt(jnp.where(lane_row < GROUPS, squares_row, 0.0) / group_count + EPS), 0.0
    )
    affine[yx, :, 2 * padded :] = jnp.where(
        lane_row < GROUPS, mean_row, jnp.where(lane_row < 2 * GROUPS, pltpu.roll(rstd_row, GROUPS, 1), 0.0)
    )

    others(2 * Z, member, lambda p: act_copy(member, p).wait_recv())

    own_mean = jnp.sum(own_mask[...] * mean_row, axis=1, keepdims=True)
    own_rstd = jnp.sum(own_mask[...] * rstd_row, axis=1, keepdims=True)
    own_gamma, own_beta = own_gain[0, :, :1], own_gain[1, :, :1]
    for slot in range(2 * Z):
        shaped = (act_in[slot].astype(F32) - own_mean) * own_rstd * own_gamma + own_beta
        act_in[slot] = (shaped / (1.0 + jnp.exp(-shaped))).astype(BF16)

    partial[...] = jnp.zeros(partial.shape, F32)

    def correlate(lead):
        for row in range(Z):
            low, high = max(0, row - 1), min(Z - 1, row + 1)
            count = high - low + 1
            for side in range(2):
                i = 2 * side + 2 - lead
                if not 0 <= i < KERNEL:
                    continue
                product = lax.dot_general(
                    act_in[side * Z + low : side * Z + high + 1].reshape(count * width, cells),
                    slabs[lead, row + 1],
                    (((1,), (1,)), ((), ())),
                    preferred_element_type=F32,
                )
                for n in range(count):
                    j = low + n + 1 - row
                    partial[i * KERNEL + j] += product[n * width : (n + 1) * width]

    @pl.when(takes_next)
    def _():
        def pass_next(row):
            landed(2, row)
            to_mate(2, row, 1).start()

        others(Z, zl, pass_next)

    for lead in range(3):
        correlate(lead)

    mean = jnp.sum(mask_a[...] * mean_row, axis=1, keepdims=True)
    rstd = jnp.sum(mask_a[...] * rstd_row, axis=1, keepdims=True)
    for side in range(2):
        at = pl.ds(side * half, half)
        normed = (x_ref[:, at] - mean) * rstd
        shaped = normed * gain[0] + gain[1]
        sig = 1.0 / (1.0 + jnp.exp(-shaped))
        normed_ref[:, at] = normed
        slope_ref[:, at] = sig * (1.0 + shaped * (1.0 - sig))

    @pl.when((core == 0) & (zh < Z - 1))
    def _():
        def next_from_mate(row, carry):
            landed(2, row)
            return carry

        lax.fori_loop(0, Z, next_from_mate, 0)

    fill(range(4, 6))

    gradient((0, 1))
    shaped_grad = grad_ref[...] * slope_ref[...]
    slope_ref[...] = shaped_grad
    scaled = shaped_grad * normed_ref[...]
    beta_sum = jnp.sum(shaped_grad[:, :half] + shaped_grad[:, half:], axis=1, keepdims=True)
    gamma_sum = jnp.sum(scaled[:, :half] + scaled[:, half:], axis=1, keepdims=True)
    affine[yx, :, 0:C] = jnp.broadcast_to(gamma_sum, (C, LANES)).T[:1]
    affine[yx, :, padded : padded + C] = jnp.broadcast_to(beta_sum, (C, LANES)).T[:1]
    start_affine, recv_affine, sent_affine = exchange(affine, affine_s, affine_r, YX, yx, in_plane)
    start_affine()
    groups[rank] = jnp.sum(
        gain[0] * (mask_a[...] * beta_sum + mask_b[...] * gamma_sum), axis=0, keepdims=True
    )
    for lead in range(3, 5):
        correlate(lead)

    by_owner[...] = jnp.zeros(by_owner.shape, F32)

    tile_rows = min(8, YX)
    tiles = YX // tile_rows

    def arrange(tile, carry):
        c = tile // tiles
        first_place = lax.rem(tile, tiles) * tile_rows
        at = pl.ds(pl.multiple_of(tile * tile_rows, tile_rows), tile_rows)
        for ij in range(KERNEL**2):
            for k in range(KERNEL):
                tap = ij * KERNEL + k
                values = partial[ij, at, k * LANES : (k + 1) * LANES]
                for row in range(tile_rows):
                    by_owner[(first_place + row) * 3 + c, tap : tap + 1, :] = values[row : row + 1]
        return carry

    lax.fori_loop(0, 3 * tiles, arrange, 0)
    plane_out[...] = by_owner[...].astype(BF16).reshape(plane_out.shape)

    def plane_copy(peer, slot):
        return remote(plane_out.at[peer], plane_in.at[slot], plane_s.at[peer], plane_r.at[slot], in_plane(peer))

    others(YX, yx, lambda p: plane_copy(p, yx).start())
    plane_in[yx] = jnp.zeros(plane_in.shape[1:], BF16)

    start_groups, recv_groups, sent_groups = exchange(groups, groups_s, groups_r, column, rank, in_column)
    start_groups()

    recv_affine()
    affine_rows = listed(affine)
    mean_table[...] = affine_rows[:, 2 * padded : 2 * padded + GROUPS]
    rstd_table[...] = affine_rows[:, 2 * padded + GROUPS : 2 * padded + 2 * GROUPS]
    stores = [
        pltpu.make_async_copy(source, target, store_sem.at[n])
        for n, (source, target) in enumerate(
            (
                (mean_table, mean_ref),
                (rstd_table, rstd_ref),
                (act_grad, act_grad_ref),
                (gamma_grad, gamma_grad_ref),
                (beta_grad, beta_grad_ref),
                (kernel_grad, kernel_grad_ref),
            )
        )
    ]
    stores[0].start()
    stores[1].start()
    affine_all[rank] = jnp.sum(affine_rows[:, : 2 * padded], axis=0, keepdims=True)
    start_all, recv_all, sent_all = exchange(affine_all, all_s, all_r, column, rank, in_column)
    start_all()

    others(YX, yx, lambda p: plane_copy(yx, p).wait_recv())

    def add(slot, carry):
        return carry + plane_in[slot].astype(F32)

    summed = lax.fori_loop(0, YX, add, by_owner[pl.ds(3 * yx, 3)])
    share = 3 * O // Z
    tap_lane = lax.broadcasted_iota(jnp.int32, summed.shape[1:], 1)
    for part in range(Z):
        packed = jnp.zeros(summed.shape[1:], F32)
        for c in range(3):
            low, high = max(share * part, O * c), min(share * (part + 1), O * (c + 1))
            if high <= low:
                continue
            inside = (tap_lane >= low - share * part) & (tap_lane < high - share * part)
            shift = (O * c - share * part) % LANES
            moved = pltpu.roll(summed[c], shift, 1) if shift else summed[c]
            packed = jnp.where(inside, moved, packed)
        column_out[part] = packed

    def column_copy(part, slot):
        device = (yx * (2 * Z) + zl * 2 + core, part)
        return remote(column_out.at[part], column_in.at[slot], column_s.at[part], column_r.at[slot], device)

    at_home = zh == zl

    def send_part(part, carry):
        stays = at_home & (part == zl)

        @pl.when(jnp.logical_not(stays))
        def _():
            column_copy(part, zh).start()

        @pl.when(stays)
        def _():
            column_in[zh] = column_out[part]

        return carry

    lax.fori_loop(0, Z, send_part, 0)

    recv_groups()
    group_row = jnp.sum(listed(groups), axis=0, keepdims=True) / group_count
    first = jnp.sum(mask_a[...] * group_row, axis=1, keepdims=True)
    second = jnp.sum(mask_b[...] * group_row, axis=1, keepdims=True)
    for side in range(2):
        at = pl.ds(side * half, half)
        act_grad[:, side, :] = (
            rstd * (gain[0] * slope_ref[:, at] - first - normed_ref[:, at] * second)
        ).astype(BF16)
    stores[2].start()

    recv_all()
    totals = jnp.sum(listed(affine_all), axis=0, keepdims=True) * scale
    gamma_grad[...] = totals[:, :C].reshape(C)
    beta_grad[...] = totals[:, padded : padded + C].reshape(C)
    stores[3].start()
    stores[4].start()

    sent_stats()
    for which, step in enumerate(steps):
        ring_copy(zh, which, step).wait_send()
    sent_groups()
    sent_affine()
    sent_all()

    @pl.when(gives_next)
    def _():
        block_copy_next().wait_send()

    to_line(core, line_s, wait_send)
    passed(core, 0, wait_send)

    def mate_sent(row, carry):
        to_mate(core, row, 0).wait_send()
        return carry

    lax.fori_loop(0, Z, mate_sent, 0)

    @pl.when(takes_next)
    def _():
        others(Z, zl, lambda p: block_copy(2, zl, next_line_s.at[p], (f, p)).wait_send())

        def next_sent(row, carry):
            to_mate(2, row, 1).wait_send()
            return carry

        lax.fori_loop(0, Z, next_sent, 0)

    others(2 * Z, member, lambda p: act_copy(p, member).wait_send())
    others(YX, yx, lambda p: plane_copy(p, yx).wait_send())

    def take_part(slot, carry):
        @pl.when(jnp.logical_not(at_home & (slot == zh)))
        def _():
            column_copy(0, slot).wait_recv()

        return carry

    lax.fori_loop(0, Z, take_part, 0)
    result = jnp.sum(column_in[...], axis=0) * scale
    kernel_grad[...] = result[: KERNEL**3, :share]
    stores[5].start()

    def part_sent(part, carry):
        @pl.when(jnp.logical_not(at_home & (part == zl)))
        def _():
            column_copy(part, zh).wait_send()

        return carry

    lax.fori_loop(0, Z, part_sent, 0)
    for store in stores:
        store.wait()


def hand_over(*refs):
    count = len(refs) // 3
    sources, targets, holds = refs[:count], refs[count : 2 * count], refs[2 * count : 3 * count]
    load_sem, store_sem = refs[3 * count :]
    loads = [pltpu.make_async_copy(sources[n], holds[n], load_sem.at[n]) for n in range(count)]
    stores = [pltpu.make_async_copy(holds[n], targets[n], store_sem.at[n]) for n in range(count)]
    for load in loads:
        load.start()
    for load, store in zip(loads, stores):
        load.wait()
        store.start()
    for store in stores:
        store.wait()


def on_device(Z, YX, act, cotangent, kernel, gamma, beta):
    C, frames, rows, half = act.shape
    O = cotangent.shape[0]
    cells = frames * rows * half
    column = 2 * Z * Z
    group_count = C // GROUPS * cells * column
    scale = float(cells * column * YX) ** (-0.5)
    padded = -(-C // LANES) * LANES
    sizes = (Z, YX, C, O, group_count, scale)
    hbm = pl.BlockSpec(memory_space=pl.ANY)
    dma = pltpu.SemaphoreType.DMA
    width = 3 * YX
    outputs = (
        jax.ShapeDtypeStruct((C, frames, half), BF16),
        jax.ShapeDtypeStruct((KERNEL**3, 3 * O // Z), F32),
        jax.ShapeDtypeStruct((C,), F32),
        jax.ShapeDtypeStruct((C,), F32),
        jax.ShapeDtypeStruct((YX, GROUPS), F32),
        jax.ShapeDtypeStruct((YX, GROUPS), F32),
    )
    scratch = [
        pltpu.VMEM((C, frames, half), BF16),
        pltpu.VMEM((O, frames, half), BF16),
        pltpu.VMEM((C,), F32),
        pltpu.VMEM((C,), F32),
        *(pltpu.VMEM(out.shape, out.dtype) for out in outputs),
        pltpu.VMEM((C, cells), F32),
        pltpu.VMEM((2 * Z, 1, LANES), F32),
        pltpu.VMEM((Z, 1, LANES), F32),
        pltpu.VMEM((column, 1, LANES), F32),
        pltpu.VMEM((YX, 1, 2 * padded + LANES), F32),
        pltpu.VMEM((column, 1, 2 * padded), F32),
        pltpu.VMEM((3, Z, O, cells), BF16),
        pltpu.VMEM((5, Z + 2, KERNEL * LANES, cells), BF16),
        pltpu.VMEM((KERNEL**3, LANES, C), BF16),
        pltpu.VMEM((C, C), BF16),
        pltpu.VMEM((C, LANES), F32),
        pltpu.VMEM((C, LANES), F32),
        pltpu.VMEM((2, C, LANES), F32),
        pltpu.VMEM((width, LANES), F32),
        pltpu.VMEM((2, width, LANES), F32),
        pltpu.VMEM((C, cells), F32),
        pltpu.VMEM((C, cells), F32),
        pltpu.VMEM((C, cells), F32),
        pltpu.VMEM((2 * Z, width, cells), BF16),
        pltpu.VMEM((2 * Z, width, cells), BF16),
        pltpu.VMEM((KERNEL**2, width, KERNEL * LANES), F32),
        pltpu.VMEM((width, 32, LANES), F32),
        pltpu.VMEM((YX, 3, 32, LANES), BF16),
        pltpu.VMEM((YX, 3, 32, LANES), BF16),
        pltpu.VMEM((Z, 32, LANES), F32),
        pltpu.VMEM((Z, 32, LANES), F32),
        dma((5,)),
        dma((6,)),
        dma((2 * Z,)),
        dma((2 * Z,)),
        dma((3,)),
        dma((Z,)),
        dma((column,)),
        dma((column,)),
        dma((YX,)),
        dma((YX,)),
        dma((column,)),
        dma((column,)),
        dma((Z,)),
        dma((2, Z)),
        dma((1,)),
        dma((Z,)),
        dma((2, Z)),
        dma((3, Z)),
        dma((2 * Z,)),
        dma((2 * Z,)),
        dma((YX,)),
        dma((YX,)),
        dma((Z,)),
        dma((Z,)),
    ]
    results = pl.pallas_call(
        functools.partial(body, sizes),
        out_shape=outputs,
        in_specs=[hbm] * 5,
        out_specs=(hbm,) * 6,
        scratch_shapes=scratch,
        compiler_params=pltpu.CompilerParams(
            collective_id=0, has_side_effects=True, vmem_limit_bytes=62 * 2**20
        ),
        name="unit_backward",
    )(
        act.reshape(C, frames, half),
        cotangent.reshape(O, frames, half),
        kernel,
        gamma,
        beta,
    )
    results = pl.pallas_call(
        hand_over,
        out_shape=outputs,
        in_specs=[hbm] * 6,
        out_specs=(hbm,) * 6,
        scratch_shapes=[*(pltpu.VMEM(out.shape, out.dtype) for out in outputs), dma((6,)), dma((6,))],
        name="hand_over",
    )(*results)
    return (results[0].reshape(act.shape), *results[1:])


def solution(mesh):
    Z = mesh.shape["rows"]
    YX = mesh.shape["frames"] // (2 * Z)
    in_specs = (P(None, "frames", "rows", None), P(None, "frames", "rows", None), P(), P(), P())
    out_specs = (P(None, "frames", "rows", None), P(None, ("frames", "rows")), P(), P(), P(), P())
    return jax.shard_map(
        functools.partial(on_device, Z, YX), mesh=mesh, in_specs=in_specs, out_specs=out_specs, check_vma=False
    )
```

```python
import functools

import jax
import jax.numpy as jnp
from jax import lax
from jax.experimental import pallas as pl
from jax.experimental.pallas import tpu as pltpu
from jax.sharding import PartitionSpec as P

GROUPS = 32
KERNEL = 3
LANES = 128
EPS = 1e-06
F32 = jnp.float32
BF16 = jnp.bfloat16
MESH = pl.DeviceIdType.MESH


def remote(src, dst, send_sem, recv_sem, device):
    return pltpu.make_async_remote_copy(
        src_ref=src,
        dst_ref=dst,
        send_sem=send_sem,
        recv_sem=recv_sem,
        device_id=device,
        device_id_type=MESH,
    )


def others(count, me, step, farthest=False):
    def body(d, carry):
        if farthest:
            d = count // 2 + (d // 2) * (1 - 2 * lax.rem(d, 2))
        step(lax.rem(me + d, count))
        return carry

    lax.fori_loop(1, count, body, 0)


def exchange(buf, send, recv, count, me, device):
    def copy(slot, peer):
        return remote(buf.at[slot], buf.at[slot], send.at[peer], recv.at[slot], device(peer))

    return (
        lambda: others(count, me, lambda p: copy(me, p).start(), True),
        lambda: others(count, me, lambda p: copy(p, p).wait_recv()),
        lambda: others(count, me, lambda p: copy(me, p).wait_send()),
    )


def listed(buf):
    return jnp.concatenate([buf[n] for n in range(buf.shape[0])], axis=0)


def body(
    sizes,
    act_ref,
    cot_ref,
    kernel_ref,
    gamma_ref,
    beta_ref,
    act_grad_ref,
    kernel_grad_ref,
    gamma_grad_ref,
    beta_grad_ref,
    mean_ref,
    rstd_ref,
    act_raw,
    cot_raw,
    gamma_raw,
    beta_raw,
    act_grad,
    kernel_grad,
    gamma_grad,
    beta_grad,
    mean_table,
    rstd_table,
    x_ref,
    stats,
    ring,
    sums,
    clip_sums,
    affine,
    blocks,
    slabs,
    weights,
    perm,
    mask_a,
    mask_b,
    gain,
    own_mask,
    own_gain,
    normed_ref,
    slope_ref,
    grad_ref,
    act_out,
    act_in,
    partial,
    by_owner,
    plane_out,
    plane_in,
    column_out,
    column_in,
    load_sem,
    store_sem,
    stats_s,
    stats_r,
    ring_s,
    ring_r,
    sums_s,
    sums_r,
    clip_sums_s,
    clip_sums_r,
    affine_s,
    affine_r,
    line_s,
    mate_s,
    next_s,
    next_line_s,
    pass_s,
    blocks_r,
    act_s,
    act_r,
    plane_s,
    plane_r,
    column_s,
    column_r,
):
    Z, YX, C, O, group_count, scale = sizes
    per_group = C // GROUPS
    half = act_raw.shape[2]
    cells = 2 * half
    width = 3 * YX
    padded = (affine.shape[2] - LANES) // 2
    f = lax.axis_index("frames")
    zl = lax.axis_index("rows")
    core = lax.rem(f, 2)
    zh = lax.rem(f // 2, Z)
    yx = f // (2 * Z)
    member = core * Z + zl

    def in_plane(p):
        return (p * (2 * Z) + lax.rem(f, 2 * Z), zl)

    def in_block(p):
        return (yx * (2 * Z) + zh * 2 + p // Z, lax.rem(p, Z))

    mate = (f + 1 - 2 * core, zl)

    def across_blocks(step):
        return (yx * (2 * Z) + lax.rem(zh + step + Z, Z) * 2 + core, zl)

    partner = (yx * (2 * Z) + lax.rem(zh + 2 * core - 1 + Z, Z) * 2 + 1 - core, zl)
    steps = [Z // 2] + [step for n in range(1, Z // 2) for step in (n, -n)]

    barrier = pltpu.get_barrier_semaphore()

    def greet(device):
        pl.semaphore_signal(barrier, inc=1, device_id=device, device_id_type=MESH)

    for step in steps:
        greet(across_blocks(step))
    greet(partner)
    others(YX, yx, lambda p: greet(in_plane(p)), True)
    others(2 * Z, member, lambda p: greet(in_block(p)))

    loads = [
        pltpu.make_async_copy(source, target, load_sem.at[n])
        for n, (source, target) in enumerate(
            (
                (act_ref, act_raw),
                (cot_ref, cot_raw),
                (gamma_ref, gamma_raw),
                (beta_ref, beta_raw),
                (kernel_ref, weights.at[:, pl.ds(0, O), :]),
            )
        )
    ]
    for load in loads:
        load.start()

    chan = lax.broadcasted_iota(jnp.int32, (C, LANES), 0)
    lane = lax.broadcasted_iota(jnp.int32, (C, LANES), 1)
    first_chan = lane * per_group
    mask_a[...] = jnp.where((chan >= first_chan) & (chan < first_chan + per_group), 1.0, 0.0).astype(F32)
    place = lax.broadcasted_iota(jnp.int32, (YX, C), 0) * (6 * Z)
    source = lax.broadcasted_iota(jnp.int32, (YX, C), 1)
    for p in range(2 * Z):
        for c in range(3):
            base = p * width + c * YX
            offset = (p % Z) * 6 + (p // Z) * 3 + c
            perm[base : base + YX, :] = jnp.where(source == place + offset, 1.0, 0.0).astype(BF16)

    loads[0].wait()
    x_a = act_raw[:, 0, :].astype(F32)
    x_b = act_raw[:, 1, :].astype(F32)
    x_ref[:, :half] = x_a
    x_ref[:, half:] = x_b
    mean = jnp.sum(x_a + x_b, axis=1, keepdims=True) / cells
    squares = jnp.sum((x_a - mean) * (x_a - mean) + (x_b - mean) * (x_b - mean), axis=1, keepdims=True)
    mean_row = jnp.sum(mask_a[...] * mean, axis=0, keepdims=True) / per_group
    gap = mean - jnp.sum(mask_a[...] * mean_row, axis=1, keepdims=True)
    squares = squares + cells * (gap * gap)
    stats[member] = mean_row + pltpu.roll(jnp.sum(mask_a[...] * squares, axis=0, keepdims=True), GROUPS, 1)

    loads[1].wait()
    for side in range(2):
        blocks[core, zl, :, side * half : (side + 1) * half] = cot_raw[:, side, :].astype(F32).astype(BF16)

    ordered = jnp.dot(perm[...], x_ref[...].astype(BF16), preferred_element_type=F32).astype(BF16)
    act_out[...] = ordered.reshape(act_out.shape)
    act_in[member] = act_out[member]

    pl.semaphore_wait(barrier, len(steps) + 1 + YX - 1 + 2 * Z - 1)

    def block_copy(pair, row, send, device):
        ref = blocks.at[pair, row]
        return remote(ref, ref, send, blocks_r.at[pair, row], device)

    side_rows = Z // 2
    own_half = zl // side_rows
    gateway = side_rows - own_half
    is_gateway = zl == side_rows - 1 + own_half

    def half_peers(step):
        others(side_rows, lax.rem(zl, side_rows), lambda n: step(own_half * side_rows + n))

    def to_line(pair, sems, act):
        half_peers(lambda p: act(block_copy(pair, zl, sems.at[p], (f, p))))
        act(block_copy(pair, zl, sems.at[gateway], (f, gateway)))

    def to_mate(pair, row, which):
        return block_copy(pair, row, mate_s.at[which, row], mate)

    def landed(pair, row):
        block_copy(pair, row, line_s.at[0], mate).wait_recv()

    def start(copy):
        copy.start()

    def wait_send(copy):
        copy.wait_send()

    def passed(pair, which, act):
        @pl.when(is_gateway)
        def _():
            def across(n, carry):
                row = (1 - own_half) * side_rows + n
                half_peers(lambda p: act(block_copy(pair, row, pass_s.at[which, row], (f, p))))
                return carry

            lax.fori_loop(0, side_rows, across, 0)

    def take_line(pair, which):
        def across(n, carry):
            row = (1 - own_half) * side_rows + n
            landed(pair, row)

            @pl.when(is_gateway)
            def _():
                half_peers(lambda p: block_copy(pair, row, pass_s.at[which, row], (f, p)).start())

            to_mate(pair, row, which).start()
            return carry

        def near():
            def step(p):
                landed(pair, p)
                to_mate(pair, p, which).start()

            half_peers(step)

        def far():
            lax.fori_loop(0, side_rows, across, 0)

        near()
        far()

    gives_next = (core == 0) & (zh > 0)
    takes_next = (core == 1) & (zh < Z - 1)
    earlier = (lax.max(f - 1, 0), zl)

    def block_copy_next():
        return remote(blocks.at[core, zl], blocks.at[2, zl], next_s.at[0], blocks_r.at[2, zl], earlier)

    @pl.when(gives_next)
    def _():
        block_copy_next().start()

    start_stats, recv_stats, sent_stats = exchange(stats, stats_s, stats_r, 2 * Z, member, in_block)
    start_stats()
    to_line(core, line_s, start)
    to_mate(core, zl, 0).start()

    def act_copy(peer, slot):
        return remote(act_out.at[peer], act_in.at[slot], act_s.at[peer], act_r.at[slot], in_block(peer))


    first_chan = (lane - GROUPS) * per_group
    mask_b[...] = jnp.where((chan >= first_chan) & (chan < first_chan + per_group), 1.0, 0.0).astype(F32)
    loads[2].wait()
    loads[3].wait()
    gamma_row = gamma_raw[...].reshape(1, C)
    beta_row = beta_raw[...].reshape(1, C)
    gain[0] = jnp.broadcast_to(gamma_row, (LANES, C)).T
    gain[1] = jnp.broadcast_to(beta_row, (LANES, C)).T
    own_chan = lax.broadcasted_iota(jnp.int32, (YX, LANES), 0) * (6 * Z)
    own_lane = lax.broadcasted_iota(jnp.int32, (YX, LANES), 1) * per_group
    for c in range(3):
        at = pl.ds(c * YX, YX)
        offset = zl * 6 + core * 3 + c
        chosen = jnp.where(source == place + offset, 1.0, 0.0).astype(F32)
        own_gain[0, at, :] = jnp.broadcast_to(jnp.sum(chosen * gamma_row, axis=1, keepdims=True), (YX, LANES))
        own_gain[1, at, :] = jnp.broadcast_to(jnp.sum(chosen * beta_row, axis=1, keepdims=True), (YX, LANES))
        inside = (own_chan + offset >= own_lane) & (own_chan + offset < own_lane + per_group)
        own_mask[at, :] = jnp.where(inside, 1.0, 0.0).astype(F32)

    if O < LANES:
        weights[:, O:, :] = jnp.zeros((KERNEL**3, LANES - O, C), BF16)

    @pl.when(zh == Z - 1)
    def _():
        blocks[2] = jnp.zeros(blocks.shape[1:], BF16)

    slabs[:, 0] = jnp.zeros((5,) + slabs.shape[2:], BF16)
    slabs[:, Z + 1] = jnp.zeros((5,) + slabs.shape[2:], BF16)
    if O < LANES:
        for k in range(KERNEL):
            slabs[:, 1 : Z + 1, k * LANES + O : (k + 1) * LANES, :] = jnp.zeros((5, Z, LANES - O, cells), BF16)

    lane_row = lax.broadcasted_iota(jnp.int32, (1, LANES), 1)

    def combined(rows, cells_of_one):
        total = jnp.sum(rows, axis=0, keepdims=True)
        mean_row = jnp.where(lane_row < GROUPS, total / rows.shape[0], 0.0)
        gaps = jnp.where(lane_row < GROUPS, rows - mean_row, 0.0)
        return mean_row, pltpu.roll(total, LANES - GROUPS, 1) + cells_of_one * jnp.sum(gaps * gaps, axis=0, keepdims=True)

    recv_stats()
    block_mean, block_squares = combined(listed(stats), per_group * cells)
    ring[zh] = block_mean + pltpu.roll(jnp.where(lane_row < GROUPS, block_squares, 0.0), GROUPS, 1)

    def ring_copy(slot, which, step):
        return remote(ring.at[slot], ring.at[slot], ring_s.at[which], ring_r.at[slot], across_blocks(step))

    def block_at(step):
        return lax.rem(zh + step + Z, Z)

    for which, step in enumerate(steps):
        ring_copy(zh, which, step).start()

    @pl.when(takes_next)
    def _():
        landed(2, zl)
        to_line(2, next_line_s, start)
        to_mate(2, zl, 1).start()

    others(2 * Z, member, lambda p: act_copy(p, member).start())

    take_line(core, 0)

    def from_mate(row, carry):
        landed(1 - core, row)
        return carry

    lax.fori_loop(0, Z, from_mate, 0)

    column_lane = lax.broadcasted_iota(jnp.int32, (O, half), 1)

    def fill(frames):
        def fill_row(row, carry):
            for frame in frames:
                slab = blocks[frame // 2, row, :, (frame % 2) * half : (frame % 2 + 1) * half]
                wide = slab.astype(F32)
                shifted = (
                    jnp.where(column_lane < half - 1, pltpu.roll(wide, half - 1, 1), 0.0).astype(BF16),
                    slab,
                    jnp.where(column_lane > 0, pltpu.roll(wide, 1, 1), 0.0).astype(BF16),
                )
                for k in range(KERNEL):
                    if frame < 5:
                        slabs[frame, row + 1, k * LANES : k * LANES + O, :half] = shifted[k]
                    if frame > 0:
                        slabs[frame - 1, row + 1, k * LANES : k * LANES + O, half:] = shifted[k]
            return carry

        lax.fori_loop(0, Z, fill_row, 0)

    fill(range(4))

    def gradient(lags):
        total = grad_ref[...]
        for i in lags:
            for j in range(KERNEL):
                tap = (i * KERNEL + j) * KERNEL
                total += lax.dot_general(
                    weights[tap : tap + KERNEL].reshape(KERNEL * LANES, C),
                    slabs[2 * core + 2 - i, zl - j + 2],
                    (((0,), (0,)), ((), ())),
                    preferred_element_type=F32,
                )
        grad_ref[...] = total

    loads[4].wait()
    grad_ref[...] = jnp.zeros((C, cells), F32)
    gradient((2,))


    @pl.when(takes_next)
    def _():
        take_line(2, 1)

    for step in steps:
        ring_copy(block_at(step), 0, step).wait_recv()
    mean_row, squares_row = combined(listed(ring), 2 * Z * per_group * cells)
    rstd_row = jnp.where(
        lane_row < GROUPS, lax.rsqrt(jnp.where(lane_row < GROUPS, squares_row, 0.0) / group_count + EPS), 0.0
    )
    affine[yx, :, 2 * padded :] = jnp.where(
        lane_row < GROUPS, mean_row, jnp.where(lane_row < 2 * GROUPS, pltpu.roll(rstd_row, GROUPS, 1), 0.0)
    )

    others(2 * Z, member, lambda p: act_copy(member, p).wait_recv())

    own_mean = jnp.sum(own_mask[...] * mean_row, axis=1, keepdims=True)
    own_rstd = jnp.sum(own_mask[...] * rstd_row, axis=1, keepdims=True)
    own_gamma, own_beta = own_gain[0, :, :1], own_gain[1, :, :1]
    for slot in range(2 * Z):
        shaped = (act_in[slot].astype(F32) - own_mean) * own_rstd * own_gamma + own_beta
        act_in[slot] = (shaped / (1.0 + jnp.exp(-shaped))).astype(BF16)

    partial[...] = jnp.zeros(partial.shape, F32)

    def correlate(lead):
        for row in range(Z):
            low, high = max(0, row - 1), min(Z - 1, row + 1)
            count = high - low + 1
            for side in range(2):
                i = 2 * side + 2 - lead
                if not 0 <= i < KERNEL:
                    continue
                product = lax.dot_general(
                    act_in[side * Z + low : side * Z + high + 1].reshape(count * width, cells),
                    slabs[lead, row + 1],
                    (((1,), (1,)), ((), ())),
                    preferred_element_type=F32,
                )
                for n in range(count):
                    j = low + n + 1 - row
                    partial[i * KERNEL + j] += product[n * width : (n + 1) * width]

    for lead in range(3):
        correlate(lead)

    mean = jnp.sum(mask_a[...] * mean_row, axis=1, keepdims=True)
    rstd = jnp.sum(mask_a[...] * rstd_row, axis=1, keepdims=True)
    for side in range(2):
        at = pl.ds(side * half, half)
        normed = (x_ref[:, at] - mean) * rstd
        shaped = normed * gain[0] + gain[1]
        sig = 1.0 / (1.0 + jnp.exp(-shaped))
        normed_ref[:, at] = normed
        slope_ref[:, at] = sig * (1.0 + shaped * (1.0 - sig))

    @pl.when((core == 0) & (zh < Z - 1))
    def _():
        def next_from_mate(row, carry):
            landed(2, row)
            return carry

        lax.fori_loop(0, Z, next_from_mate, 0)

    fill(range(4, 6))

    gradient((0, 1))
    shaped_grad = grad_ref[...] * slope_ref[...]
    slope_ref[...] = shaped_grad
    scaled = shaped_grad * normed_ref[...]
    beta_sum = jnp.sum(shaped_grad[:, :half] + shaped_grad[:, half:], axis=1, keepdims=True)
    gamma_sum = jnp.sum(scaled[:, :half] + scaled[:, half:], axis=1, keepdims=True)
    sums[member, :, 0:C] = jnp.broadcast_to(gamma_sum, (C, LANES)).T[:1]
    sums[member, :, padded : padded + C] = jnp.broadcast_to(beta_sum, (C, LANES)).T[:1]
    sums[member, :, 2 * padded :] = jnp.sum(
        gain[0] * (mask_a[...] * beta_sum + mask_b[...] * gamma_sum), axis=0, keepdims=True
    )
    start_sums, recv_sums, sent_sums = exchange(sums, sums_s, sums_r, 2 * Z, member, in_block)
    start_sums()

    for lead in range(3, 5):
        correlate(lead)

    by_owner[...] = jnp.zeros(by_owner.shape, F32)

    tile_rows = min(8, YX)
    tiles = YX // tile_rows

    def arrange(tile, carry):
        c = tile // tiles
        first_place = lax.rem(tile, tiles) * tile_rows
        at = pl.ds(pl.multiple_of(tile * tile_rows, tile_rows), tile_rows)
        for ij in range(KERNEL**2):
            for k in range(KERNEL):
                tap = ij * KERNEL + k
                values = partial[ij, at, k * LANES : (k + 1) * LANES]
                for row in range(tile_rows):
                    by_owner[(first_place + row) * 3 + c, tap : tap + 1, :] = values[row : row + 1]
        return carry

    lax.fori_loop(0, 3 * tiles, arrange, 0)
    plane_out[...] = by_owner[...].astype(BF16).reshape(plane_out.shape)

    def plane_copy(peer, slot):
        return remote(plane_out.at[peer], plane_in.at[slot], plane_s.at[peer], plane_r.at[slot], in_plane(peer))

    others(YX, yx, lambda p: plane_copy(p, yx).start())
    plane_in[yx] = jnp.zeros(plane_in.shape[1:], BF16)

    recv_sums()
    clip_sums[zh] = jnp.sum(listed(sums), axis=0, keepdims=True)

    def sums_copy(slot, which, step):
        return remote(
            clip_sums.at[slot], clip_sums.at[slot], clip_sums_s.at[which], clip_sums_r.at[slot], across_blocks(step)
        )

    for which, step in enumerate(steps):
        sums_copy(zh, which, step).start()

    others(YX, yx, lambda p: plane_copy(yx, p).wait_recv())

    def add(slot, carry):
        return carry + plane_in[slot].astype(F32)

    summed = lax.fori_loop(0, YX, add, by_owner[pl.ds(3 * yx, 3)])
    share = 3 * O // Z
    tap_lane = lax.broadcasted_iota(jnp.int32, summed.shape[1:], 1)
    for part in range(Z):
        packed = jnp.zeros(summed.shape[1:], F32)
        for c in range(3):
            low, high = max(share * part, O * c), min(share * (part + 1), O * (c + 1))
            if high <= low:
                continue
            inside = (tap_lane >= low - share * part) & (tap_lane < high - share * part)
            shift = (O * c - share * part) % LANES
            moved = pltpu.roll(summed[c], shift, 1) if shift else summed[c]
            packed = jnp.where(inside, moved, packed)
        column_out[part] = packed

    def column_copy(part, slot):
        device = (yx * (2 * Z) + zl * 2 + core, part)
        return remote(column_out.at[part], column_in.at[slot], column_s.at[part], column_r.at[slot], device)

    at_home = zh == zl

    def send_part(part, carry):
        stays = at_home & (part == zl)

        @pl.when(jnp.logical_not(stays))
        def _():
            column_copy(part, zh).start()

        @pl.when(stays)
        def _():
            column_in[zh] = column_out[part]

        return carry

    lax.fori_loop(0, Z, send_part, 0)

    for step in steps:
        sums_copy(block_at(step), 0, step).wait_recv()
    clip_total = jnp.sum(listed(clip_sums), axis=0, keepdims=True)
    affine[yx, :, : 2 * padded] = clip_total[:, : 2 * padded]
    start_affine, recv_affine, sent_affine = exchange(affine, affine_s, affine_r, YX, yx, in_plane)
    start_affine()

    group_row = clip_total[:, 2 * padded :] / group_count
    first = jnp.sum(mask_a[...] * group_row, axis=1, keepdims=True)
    second = jnp.sum(mask_b[...] * group_row, axis=1, keepdims=True)
    for side in range(2):
        at = pl.ds(side * half, half)
        act_grad[:, side, :] = (
            rstd * (gain[0] * slope_ref[:, at] - first - normed_ref[:, at] * second)
        ).astype(BF16)

    stores = [
        pltpu.make_async_copy(source, target, store_sem.at[n])
        for n, (source, target) in enumerate(
            (
                (act_grad, act_grad_ref),
                (mean_table, mean_ref),
                (rstd_table, rstd_ref),
                (gamma_grad, gamma_grad_ref),
                (beta_grad, beta_grad_ref),
                (kernel_grad, kernel_grad_ref),
            )
        )
    ]
    stores[0].start()

    recv_affine()
    affine_rows = listed(affine)
    mean_table[...] = affine_rows[:, 2 * padded : 2 * padded + GROUPS]
    rstd_table[...] = affine_rows[:, 2 * padded + GROUPS : 2 * padded + 2 * GROUPS]
    stores[1].start()
    stores[2].start()
    totals = jnp.sum(affine_rows[:, : 2 * padded], axis=0, keepdims=True) * scale
    gamma_grad[...] = totals[:, :C].reshape(C)
    beta_grad[...] = totals[:, padded : padded + C].reshape(C)
    stores[3].start()
    stores[4].start()

    sent_stats()
    for which, step in enumerate(steps):
        ring_copy(zh, which, step).wait_send()
    sent_sums()
    for which, step in enumerate(steps):
        sums_copy(zh, which, step).wait_send()
    sent_affine()

    @pl.when(gives_next)
    def _():
        block_copy_next().wait_send()

    to_line(core, line_s, wait_send)
    passed(core, 0, wait_send)

    def mate_sent(row, carry):
        to_mate(core, row, 0).wait_send()
        return carry

    lax.fori_loop(0, Z, mate_sent, 0)

    @pl.when(takes_next)
    def _():
        to_line(2, next_line_s, wait_send)
        passed(2, 1, wait_send)

        def next_sent(row, carry):
            to_mate(2, row, 1).wait_send()
            return carry

        lax.fori_loop(0, Z, next_sent, 0)

    others(2 * Z, member, lambda p: act_copy(p, member).wait_send())
    others(YX, yx, lambda p: plane_copy(p, yx).wait_send())

    def take_part(slot, carry):
        @pl.when(jnp.logical_not(at_home & (slot == zh)))
        def _():
            column_copy(0, slot).wait_recv()

        return carry

    lax.fori_loop(0, Z, take_part, 0)
    result = jnp.sum(column_in[...], axis=0) * scale
    kernel_grad[...] = result[: KERNEL**3, :share]
    stores[5].start()

    def part_sent(part, carry):
        @pl.when(jnp.logical_not(at_home & (part == zl)))
        def _():
            column_copy(part, zh).wait_send()

        return carry

    lax.fori_loop(0, Z, part_sent, 0)
    for store in stores:
        store.wait()


def hand_over(*refs):
    count = len(refs) // 3
    sources, targets, holds = refs[:count], refs[count : 2 * count], refs[2 * count : 3 * count]
    load_sem, store_sem = refs[3 * count :]
    loads = [pltpu.make_async_copy(sources[n], holds[n], load_sem.at[n]) for n in range(count)]
    stores = [pltpu.make_async_copy(holds[n], targets[n], store_sem.at[n]) for n in range(count)]
    for load in loads:
        load.start()
    for load, store in zip(loads, stores):
        load.wait()
        store.start()
    for store in stores:
        store.wait()


def on_device(Z, YX, act, cotangent, kernel, gamma, beta):
    C, frames, rows, half = act.shape
    O = cotangent.shape[0]
    cells = frames * rows * half
    column = 2 * Z * Z
    group_count = C // GROUPS * cells * column
    scale = float(cells * column * YX) ** (-0.5)
    padded = -(-C // LANES) * LANES
    sizes = (Z, YX, C, O, group_count, scale)
    hbm = pl.BlockSpec(memory_space=pl.ANY)
    dma = pltpu.SemaphoreType.DMA
    width = 3 * YX
    outputs = (
        jax.ShapeDtypeStruct((C, frames, half), BF16),
        jax.ShapeDtypeStruct((KERNEL**3, 3 * O // Z), F32),
        jax.ShapeDtypeStruct((C,), F32),
        jax.ShapeDtypeStruct((C,), F32),
        jax.ShapeDtypeStruct((YX, GROUPS), F32),
        jax.ShapeDtypeStruct((YX, GROUPS), F32),
    )
    scratch = [
        pltpu.VMEM((C, frames, half), BF16),
        pltpu.VMEM((O, frames, half), BF16),
        pltpu.VMEM((C,), F32),
        pltpu.VMEM((C,), F32),
        *(pltpu.VMEM(out.shape, out.dtype) for out in outputs),
        pltpu.VMEM((C, cells), F32),
        pltpu.VMEM((2 * Z, 1, LANES), F32),
        pltpu.VMEM((Z, 1, LANES), F32),
        pltpu.VMEM((2 * Z, 1, 2 * padded + LANES), F32),
        pltpu.VMEM((Z, 1, 2 * padded + LANES), F32),
        pltpu.VMEM((YX, 1, 2 * padded + LANES), F32),
        pltpu.VMEM((3, Z, O, cells), BF16),
        pltpu.VMEM((5, Z + 2, KERNEL * LANES, cells), BF16),
        pltpu.VMEM((KERNEL**3, LANES, C), BF16),
        pltpu.VMEM((C, C), BF16),
        pltpu.VMEM((C, LANES), F32),
        pltpu.VMEM((C, LANES), F32),
        pltpu.VMEM((2, C, LANES), F32),
        pltpu.VMEM((width, LANES), F32),
        pltpu.VMEM((2, width, LANES), F32),
        pltpu.VMEM((C, cells), F32),
        pltpu.VMEM((C, cells), F32),
        pltpu.VMEM((C, cells), F32),
        pltpu.VMEM((2 * Z, width, cells), BF16),
        pltpu.VMEM((2 * Z, width, cells), BF16),
        pltpu.VMEM((KERNEL**2, width, KERNEL * LANES), F32),
        pltpu.VMEM((width, 32, LANES), F32),
        pltpu.VMEM((YX, 3, 32, LANES), BF16),
        pltpu.VMEM((YX, 3, 32, LANES), BF16),
        pltpu.VMEM((Z, 32, LANES), F32),
        pltpu.VMEM((Z, 32, LANES), F32),
        dma((5,)),
        dma((6,)),
        dma((2 * Z,)),
        dma((2 * Z,)),
        dma((Z,)),
        dma((Z,)),
        dma((2 * Z,)),
        dma((2 * Z,)),
        dma((Z,)),
        dma((Z,)),
        dma((YX,)),
        dma((YX,)),
        dma((Z,)),
        dma((2, Z)),
        dma((1,)),
        dma((Z,)),
        dma((2, Z)),
        dma((3, Z)),
        dma((2 * Z,)),
        dma((2 * Z,)),
        dma((YX,)),
        dma((YX,)),
        dma((Z,)),
        dma((Z,)),
    ]
    results = pl.pallas_call(
        functools.partial(body, sizes),
        out_shape=outputs,
        in_specs=[hbm] * 5,
        out_specs=(hbm,) * 6,
        scratch_shapes=scratch,
        compiler_params=pltpu.CompilerParams(
            collective_id=0, has_side_effects=True, vmem_limit_bytes=62 * 2**20
        ),
        name="unit_backward",
    )(
        act.reshape(C, frames, half),
        cotangent.reshape(O, frames, half),
        kernel,
        gamma,
        beta,
    )
    results = pl.pallas_call(
        hand_over,
        out_shape=outputs,
        in_specs=[hbm] * 6,
        out_specs=(hbm,) * 6,
        scratch_shapes=[*(pltpu.VMEM(out.shape, out.dtype) for out in outputs), dma((6,)), dma((6,))],
        name="hand_over",
    )(*results)
    return (results[0].reshape(act.shape), *results[1:])


def solution(mesh):
    Z = mesh.shape["rows"]
    YX = mesh.shape["frames"] // (2 * Z)
    in_specs = (P(None, "frames", "rows", None), P(None, "frames", "rows", None), P(), P(), P())
    out_specs = (P(None, "frames", "rows", None), P(None, ("frames", "rows")), P(), P(), P(), P())
    return jax.shard_map(
        functools.partial(on_device, Z, YX), mesh=mesh, in_specs=in_specs, out_specs=out_specs, check_vma=False
    )
```

```python
import functools

import jax
import jax.numpy as jnp
from jax import lax
from jax.experimental import pallas as pl
from jax.experimental.pallas import tpu as pltpu
from jax.sharding import PartitionSpec as P

GROUPS = 32
KERNEL = 3
LANES = 128
EPS = 1e-06
F32 = jnp.float32
BF16 = jnp.bfloat16
MESH = pl.DeviceIdType.MESH


def remote(src, dst, send_sem, recv_sem, device):
    return pltpu.make_async_remote_copy(
        src_ref=src,
        dst_ref=dst,
        send_sem=send_sem,
        recv_sem=recv_sem,
        device_id=device,
        device_id_type=MESH,
    )


def others(count, me, step, farthest=False):
    def body(d, carry):
        if farthest:
            d = count // 2 + (d // 2) * (1 - 2 * lax.rem(d, 2))
        step(lax.rem(me + d, count))
        return carry

    lax.fori_loop(1, count, body, 0)


def exchange(buf, send, recv, count, me, device):
    def copy(slot, peer):
        return remote(buf.at[slot], buf.at[slot], send.at[peer], recv.at[slot], device(peer))

    return (
        lambda: others(count, me, lambda p: copy(me, p).start(), True),
        lambda: others(count, me, lambda p: copy(p, p).wait_recv()),
        lambda: others(count, me, lambda p: copy(me, p).wait_send()),
    )


def listed(buf):
    return jnp.concatenate([buf[n] for n in range(buf.shape[0])], axis=0)


def body(
    sizes,
    act_ref,
    cot_ref,
    kernel_ref,
    gamma_ref,
    beta_ref,
    act_grad_ref,
    kernel_grad_ref,
    gamma_grad_ref,
    beta_grad_ref,
    mean_ref,
    rstd_ref,
    act_raw,
    cot_raw,
    gamma_raw,
    beta_raw,
    act_grad,
    kernel_grad,
    gamma_grad,
    beta_grad,
    mean_table,
    rstd_table,
    x_ref,
    stats,
    ring,
    sums,
    clip_sums,
    affine,
    blocks,
    slabs,
    weights,
    perm,
    mask_a,
    mask_b,
    gain,
    own_mask,
    own_gain,
    normed_ref,
    slope_ref,
    grad_ref,
    act_out,
    act_in,
    partial,
    by_owner,
    plane_out,
    plane_in,
    column_out,
    column_in,
    line_ready,
    far_ready,
    load_sem,
    store_sem,
    stats_s,
    stats_r,
    ring_s,
    ring_r,
    sums_s,
    sums_r,
    clip_sums_s,
    clip_sums_r,
    affine_s,
    affine_r,
    line_s,
    mate_s,
    next_s,
    next_line_s,
    pass_s,
    blocks_r,
    act_s,
    act_r,
    plane_s,
    plane_r,
    column_s,
    column_r,
):
    Z, YX, C, O, group_count, scale = sizes
    per_group = C // GROUPS
    half = act_raw.shape[2]
    cells = 2 * half
    width = 3 * YX
    padded = (affine.shape[2] - LANES) // 2
    f = lax.axis_index("frames")
    zl = lax.axis_index("rows")
    core = lax.rem(f, 2)
    zh = lax.rem(f // 2, Z)
    yx = f // (2 * Z)
    member = core * Z + zl

    def in_plane(p):
        return (p * (2 * Z) + lax.rem(f, 2 * Z), zl)

    def in_block(p):
        return (yx * (2 * Z) + zh * 2 + p // Z, lax.rem(p, Z))

    mate = (f + 1 - 2 * core, zl)

    def across_blocks(step):
        return (yx * (2 * Z) + lax.rem(zh + step + Z, Z) * 2 + core, zl)

    partner = (yx * (2 * Z) + lax.rem(zh + 2 * core - 1 + Z, Z) * 2 + 1 - core, zl)
    beside = (1,) if Z == 2 else (1, -1)
    steps = beside if Z == 2 else (1, -1, 2)

    barrier = pltpu.get_barrier_semaphore()

    def greet(device):
        pl.semaphore_signal(barrier, inc=1, device_id=device, device_id_type=MESH)

    for step in beside:
        greet(across_blocks(step))
    greet(partner)
    X = 4 if YX % 4 == 0 else YX
    x, y = lax.rem(yx, X), yx // X

    def along_x(p):
        return in_plane(y * X + p)

    others(X, x, lambda p: greet(along_x(p)), True)
    others(YX // X, y, lambda p: greet(in_plane(p * X + x)), True)
    others(2 * Z, member, lambda p: greet(in_block(p)))

    loads = [
        pltpu.make_async_copy(source, target, load_sem.at[n])
        for n, (source, target) in enumerate(
            (
                (act_ref, act_raw),
                (cot_ref, cot_raw),
                (gamma_ref, gamma_raw),
                (beta_ref, beta_raw),
                (kernel_ref, weights.at[:, pl.ds(0, O), :]),
            )
        )
    ]
    for load in loads:
        load.start()

    chan = lax.broadcasted_iota(jnp.int32, (C, LANES), 0)
    lane = lax.broadcasted_iota(jnp.int32, (C, LANES), 1)
    first_chan = lane * per_group
    mask_a[...] = jnp.where((chan >= first_chan) & (chan < first_chan + per_group), 1.0, 0.0).astype(F32)
    place = lax.broadcasted_iota(jnp.int32, (YX, C), 0) * (6 * Z)
    source = lax.broadcasted_iota(jnp.int32, (YX, C), 1)
    for p in range(2 * Z):
        for c in range(3):
            base = p * width + c * YX
            offset = (p % Z) * 6 + (p // Z) * 3 + c
            perm[base : base + YX, :] = jnp.where(source == place + offset, 1.0, 0.0).astype(BF16)

    loads[0].wait()
    x_a = act_raw[:, 0, :].astype(F32)
    x_b = act_raw[:, 1, :].astype(F32)
    x_ref[:, :half] = x_a
    x_ref[:, half:] = x_b
    mean = jnp.sum(x_a + x_b, axis=1, keepdims=True) / cells
    squares = jnp.sum((x_a - mean) * (x_a - mean) + (x_b - mean) * (x_b - mean), axis=1, keepdims=True)
    mean_row = jnp.sum(mask_a[...] * mean, axis=0, keepdims=True) / per_group
    gap = mean - jnp.sum(mask_a[...] * mean_row, axis=1, keepdims=True)
    squares = squares + cells * (gap * gap)
    stats[member] = mean_row + pltpu.roll(jnp.sum(mask_a[...] * squares, axis=0, keepdims=True), GROUPS, 1)

    loads[1].wait()
    for side in range(2):
        blocks[core, zl, :, side * half : (side + 1) * half] = cot_raw[:, side, :].astype(F32).astype(BF16)

    ordered = jnp.dot(perm[...], x_ref[...].astype(BF16), preferred_element_type=F32).astype(BF16)
    act_out[...] = ordered.reshape(act_out.shape)
    act_in[member] = act_out[member]

    pl.semaphore_wait(barrier, len(beside) + 1 + X - 1 + YX // X - 1 + 2 * Z - 1)

    if Z > 2:
        pl.semaphore_signal(far_ready, inc=1, device_id=across_blocks(-1), device_id_type=MESH)

    def block_copy(pair, row, send, device):
        ref = blocks.at[pair, row]
        return remote(ref, ref, send, blocks_r.at[pair, row], device)

    side_rows = Z // 2
    own_half = zl // side_rows
    gateway = side_rows - own_half
    is_gateway = zl == side_rows - 1 + own_half

    def half_peers(step):
        others(side_rows, lax.rem(zl, side_rows), lambda n: step(own_half * side_rows + n))

    def to_line(pair, sems, act):
        half_peers(lambda p: act(block_copy(pair, zl, sems.at[p], (f, p))))
        act(block_copy(pair, zl, sems.at[gateway], (f, gateway)))

    def to_mate(pair, row, which):
        return block_copy(pair, row, mate_s.at[which, row], mate)

    def landed(pair, row):
        block_copy(pair, row, line_s.at[0], mate).wait_recv()

    def start(copy):
        copy.start()

    def wait_send(copy):
        copy.wait_send()

    def passed(pair, which, act):
        @pl.when(is_gateway)
        def _():
            def across(n, carry):
                row = (1 - own_half) * side_rows + n
                half_peers(lambda p: act(block_copy(pair, row, pass_s.at[which, row], (f, p))))
                return carry

            lax.fori_loop(0, side_rows, across, 0)

    def take_line(pair, which):
        def across(n, carry):
            row = (1 - own_half) * side_rows + n
            landed(pair, row)

            @pl.when(is_gateway)
            def _():
                half_peers(lambda p: block_copy(pair, row, pass_s.at[which, row], (f, p)).start())

            to_mate(pair, row, which).start()
            return carry

        def near():
            def step(p):
                landed(pair, p)
                to_mate(pair, p, which).start()

            half_peers(step)

        def far():
            lax.fori_loop(0, side_rows, across, 0)

        near()
        far()

    gives_next = (core == 0) & (zh > 0)
    takes_next = (core == 1) & (zh < Z - 1)
    earlier = (lax.max(f - 1, 0), zl)

    def block_copy_next():
        return remote(blocks.at[core, zl], blocks.at[2, zl], next_s.at[0], blocks_r.at[2, zl], earlier)

    @pl.when(gives_next)
    def _():
        block_copy_next().start()

    start_stats, recv_stats, sent_stats = exchange(stats, stats_s, stats_r, 2 * Z, member, in_block)
    start_stats()
    to_line(core, line_s, start)
    to_mate(core, zl, 0).start()

    def act_copy(peer, slot):
        return remote(act_out.at[peer], act_in.at[slot], act_s.at[peer], act_r.at[slot], in_block(peer))


    others(X, x, lambda p: pl.semaphore_signal(line_ready, inc=1, device_id=along_x(p), device_id_type=MESH))

    first_chan = (lane - GROUPS) * per_group
    mask_b[...] = jnp.where((chan >= first_chan) & (chan < first_chan + per_group), 1.0, 0.0).astype(F32)
    loads[2].wait()
    loads[3].wait()
    gamma_row = gamma_raw[...].reshape(1, C)
    beta_row = beta_raw[...].reshape(1, C)
    gain[0] = jnp.broadcast_to(gamma_row, (LANES, C)).T
    gain[1] = jnp.broadcast_to(beta_row, (LANES, C)).T
    own_chan = lax.broadcasted_iota(jnp.int32, (YX, LANES), 0) * (6 * Z)
    own_lane = lax.broadcasted_iota(jnp.int32, (YX, LANES), 1) * per_group
    for c in range(3):
        at = pl.ds(c * YX, YX)
        offset = zl * 6 + core * 3 + c
        chosen = jnp.where(source == place + offset, 1.0, 0.0).astype(F32)
        own_gain[0, at, :] = jnp.broadcast_to(jnp.sum(chosen * gamma_row, axis=1, keepdims=True), (YX, LANES))
        own_gain[1, at, :] = jnp.broadcast_to(jnp.sum(chosen * beta_row, axis=1, keepdims=True), (YX, LANES))
        inside = (own_chan + offset >= own_lane) & (own_chan + offset < own_lane + per_group)
        own_mask[at, :] = jnp.where(inside, 1.0, 0.0).astype(F32)

    if O < LANES:
        weights[:, O:, :] = jnp.zeros((KERNEL**3, LANES - O, C), BF16)

    @pl.when(zh == Z - 1)
    def _():
        blocks[2] = jnp.zeros(blocks.shape[1:], BF16)

    slabs[:, 0] = jnp.zeros((5,) + slabs.shape[2:], BF16)
    slabs[:, Z + 1] = jnp.zeros((5,) + slabs.shape[2:], BF16)
    if O < LANES:
        for k in range(KERNEL):
            slabs[:, 1 : Z + 1, k * LANES + O : (k + 1) * LANES, :] = jnp.zeros((5, Z, LANES - O, cells), BF16)

    partial[...] = jnp.zeros(partial.shape, F32)
    by_owner[...] = jnp.zeros(by_owner.shape, F32)

    lane_row = lax.broadcasted_iota(jnp.int32, (1, LANES), 1)

    def combined(rows, cells_of_one):
        total = jnp.sum(rows, axis=0, keepdims=True)
        mean_row = jnp.where(lane_row < GROUPS, total / rows.shape[0], 0.0)
        gaps = jnp.where(lane_row < GROUPS, rows - mean_row, 0.0)
        return mean_row, pltpu.roll(total, LANES - GROUPS, 1) + cells_of_one * jnp.sum(gaps * gaps, axis=0, keepdims=True)

    recv_stats()
    block_mean, block_squares = combined(listed(stats), per_group * cells)
    ring[zh] = block_mean + pltpu.roll(jnp.where(lane_row < GROUPS, block_squares, 0.0), GROUPS, 1)

    def ring_copy(slot, which, step):
        return remote(ring.at[slot], ring.at[slot], ring_s.at[which], ring_r.at[slot], across_blocks(step))

    def block_at(step):
        return lax.rem(zh + step + Z, Z)

    for which, step in enumerate(steps):
        if step == 2:
            pl.semaphore_wait(far_ready, 1)
        ring_copy(zh, which, step).start()

    @pl.when(takes_next)
    def _():
        landed(2, zl)
        to_line(2, next_line_s, start)
        to_mate(2, zl, 1).start()

    others(2 * Z, member, lambda p: act_copy(p, member).start())

    take_line(core, 0)

    def from_mate(row, carry):
        landed(1 - core, row)
        return carry

    lax.fori_loop(0, Z, from_mate, 0)

    column_lane = lax.broadcasted_iota(jnp.int32, (O, half), 1)

    def fill(frames):
        def fill_row(row, carry):
            for frame in frames:
                slab = blocks[frame // 2, row, :, (frame % 2) * half : (frame % 2 + 1) * half]
                wide = slab.astype(F32)
                shifted = (
                    jnp.where(column_lane < half - 1, pltpu.roll(wide, half - 1, 1), 0.0).astype(BF16),
                    slab,
                    jnp.where(column_lane > 0, pltpu.roll(wide, 1, 1), 0.0).astype(BF16),
                )
                for k in range(KERNEL):
                    if frame < 5:
                        slabs[frame, row + 1, k * LANES : k * LANES + O, :half] = shifted[k]
                    if frame > 0:
                        slabs[frame - 1, row + 1, k * LANES : k * LANES + O, half:] = shifted[k]
            return carry

        lax.fori_loop(0, Z, fill_row, 0)

    fill(range(4))

    def gradient(lags):
        total = grad_ref[...]
        for i in lags:
            for j in range(KERNEL):
                tap = (i * KERNEL + j) * KERNEL
                total += lax.dot_general(
                    weights[tap : tap + KERNEL].reshape(KERNEL * LANES, C),
                    slabs[2 * core + 2 - i, zl - j + 2],
                    (((0,), (0,)), ((), ())),
                    preferred_element_type=F32,
                )
        grad_ref[...] = total

    loads[4].wait()
    grad_ref[...] = jnp.zeros((C, cells), F32)
    gradient((2,))


    @pl.when(takes_next)
    def _():
        take_line(2, 1)

    @pl.when(core == 1)
    def _():
        fill(range(4, 6))

    gradient((0, 1))

    for step in steps:
        ring_copy(block_at(step), 0, step).wait_recv()
    mean_row, squares_row = combined(listed(ring), 2 * Z * per_group * cells)
    rstd_row = jnp.where(
        lane_row < GROUPS, lax.rsqrt(jnp.where(lane_row < GROUPS, squares_row, 0.0) / group_count + EPS), 0.0
    )
    affine[yx, :, 2 * padded :] = jnp.where(
        lane_row < GROUPS, mean_row, jnp.where(lane_row < 2 * GROUPS, pltpu.roll(rstd_row, GROUPS, 1), 0.0)
    )

    others(2 * Z, member, lambda p: act_copy(member, p).wait_recv())

    own_mean = jnp.sum(own_mask[...] * mean_row, axis=1, keepdims=True)
    own_rstd = jnp.sum(own_mask[...] * rstd_row, axis=1, keepdims=True)
    own_gamma, own_beta = own_gain[0, :, :1], own_gain[1, :, :1]
    for slot in range(2 * Z):
        shaped = (act_in[slot].astype(F32) - own_mean) * own_rstd * own_gamma + own_beta
        act_in[slot] = (shaped / (1.0 + jnp.exp(-shaped))).astype(BF16)


    def correlate(lead):
        for row in range(Z):
            low, high = max(0, row - 1), min(Z - 1, row + 1)
            count = high - low + 1
            for side in range(2):
                i = 2 * side + 2 - lead
                if not 0 <= i < KERNEL:
                    continue
                product = lax.dot_general(
                    act_in[side * Z + low : side * Z + high + 1].reshape(count * width, cells),
                    slabs[lead, row + 1],
                    (((1,), (1,)), ((), ())),
                    preferred_element_type=F32,
                )
                for n in range(count):
                    j = low + n + 1 - row
                    partial[i * KERNEL + j] += product[n * width : (n + 1) * width]

    for lead in range(3):
        correlate(lead)

    mean = jnp.sum(mask_a[...] * mean_row, axis=1, keepdims=True)
    rstd = jnp.sum(mask_a[...] * rstd_row, axis=1, keepdims=True)
    for side in range(2):
        at = pl.ds(side * half, half)
        normed = (x_ref[:, at] - mean) * rstd
        shaped = normed * gain[0] + gain[1]
        sig = 1.0 / (1.0 + jnp.exp(-shaped))
        normed_ref[:, at] = normed
        slope_ref[:, at] = sig * (1.0 + shaped * (1.0 - sig))

    shaped_grad = grad_ref[...] * slope_ref[...]
    slope_ref[...] = shaped_grad
    scaled = shaped_grad * normed_ref[...]
    beta_sum = jnp.sum(shaped_grad[:, :half] + shaped_grad[:, half:], axis=1, keepdims=True)
    gamma_sum = jnp.sum(scaled[:, :half] + scaled[:, half:], axis=1, keepdims=True)
    sums[member, :, 0:C] = jnp.broadcast_to(gamma_sum, (C, LANES)).T[:1]
    sums[member, :, padded : padded + C] = jnp.broadcast_to(beta_sum, (C, LANES)).T[:1]
    sums[member, :, 2 * padded :] = jnp.sum(
        gain[0] * (mask_a[...] * beta_sum + mask_b[...] * gamma_sum), axis=0, keepdims=True
    )
    start_sums, recv_sums, sent_sums = exchange(sums, sums_s, sums_r, 2 * Z, member, in_block)
    start_sums()

    tile_rows = min(8, YX)
    tiles = YX // tile_rows

    def arrange(lags):
        lax.fori_loop(0, 3 * tiles, functools.partial(arrange_tile, lags), 0)

    def arrange_tile(lags, tile, carry):
        c = tile // tiles
        first_place = lax.rem(tile, tiles) * tile_rows
        at = pl.ds(pl.multiple_of(tile * tile_rows, tile_rows), tile_rows)
        for ij in [i * KERNEL + j for i in lags for j in range(KERNEL)]:
            for k in range(KERNEL):
                tap = ij * KERNEL + k
                values = partial[ij, at, k * LANES : (k + 1) * LANES]
                for row in range(tile_rows):
                    by_owner[(first_place + row) * 3 + c, tap : tap + 1, :] = values[row : row + 1]
        return carry

    arrange((2,))

    @pl.when((core == 0) & (zh < Z - 1))
    def _():
        def next_from_mate(row, carry):
            landed(2, row)
            return carry

        lax.fori_loop(0, Z, next_from_mate, 0)

    @pl.when(core == 0)
    def _():
        fill(range(4, 6))

    for lead in range(3, 5):
        correlate(lead)


    arrange((0, 1))
    plane_out[...] = by_owner[...].astype(BF16).reshape(plane_out.shape)

    def plane_copy(peer, slot):
        return remote(plane_out.at[peer], plane_in.at[slot], plane_s.at[peer], plane_r.at[slot], in_plane(peer))

    pl.semaphore_wait(line_ready, X - 1)
    others(YX, yx, lambda p: plane_copy(p, yx).start())
    plane_in[yx] = jnp.zeros(plane_in.shape[1:], BF16)

    recv_sums()
    clip_sums[zh] = jnp.sum(listed(sums), axis=0, keepdims=True)

    def sums_copy(slot, which, step):
        return remote(
            clip_sums.at[slot], clip_sums.at[slot], clip_sums_s.at[which], clip_sums_r.at[slot], across_blocks(step)
        )

    for which, step in enumerate(steps):
        sums_copy(zh, which, step).start()

    others(YX, yx, lambda p: plane_copy(yx, p).wait_recv())

    def add(slot, carry):
        return carry + plane_in[slot].astype(F32)

    summed = lax.fori_loop(0, YX, add, by_owner[pl.ds(3 * yx, 3)])
    share = 3 * O // Z
    tap_lane = lax.broadcasted_iota(jnp.int32, summed.shape[1:], 1)
    for part in range(Z):
        packed = jnp.zeros(summed.shape[1:], F32)
        for c in range(3):
            low, high = max(share * part, O * c), min(share * (part + 1), O * (c + 1))
            if high <= low:
                continue
            inside = (tap_lane >= low - share * part) & (tap_lane < high - share * part)
            shift = (O * c - share * part) % LANES
            moved = pltpu.roll(summed[c], shift, 1) if shift else summed[c]
            packed = jnp.where(inside, moved, packed)
        column_out[part] = packed

    def column_copy(part, slot):
        device = (yx * (2 * Z) + zl * 2 + core, part)
        return remote(column_out.at[part], column_in.at[slot], column_s.at[part], column_r.at[slot], device)

    at_home = zh == zl

    def send_part(part, carry):
        stays = at_home & (part == zl)

        @pl.when(jnp.logical_not(stays))
        def _():
            column_copy(part, zh).start()

        @pl.when(stays)
        def _():
            column_in[zh] = column_out[part]

        return carry

    lax.fori_loop(0, Z, send_part, 0)

    for step in steps:
        sums_copy(block_at(step), 0, step).wait_recv()
    clip_total = jnp.sum(listed(clip_sums), axis=0, keepdims=True)
    affine[yx, :, : 2 * padded] = clip_total[:, : 2 * padded]
    start_affine, recv_affine, sent_affine = exchange(affine, affine_s, affine_r, YX, yx, in_plane)
    start_affine()

    group_row = clip_total[:, 2 * padded :] / group_count
    first = jnp.sum(mask_a[...] * group_row, axis=1, keepdims=True)
    second = jnp.sum(mask_b[...] * group_row, axis=1, keepdims=True)
    for side in range(2):
        at = pl.ds(side * half, half)
        act_grad[:, side, :] = (
            rstd * (gain[0] * slope_ref[:, at] - first - normed_ref[:, at] * second)
        ).astype(BF16)

    stores = [
        pltpu.make_async_copy(source, target, store_sem.at[n])
        for n, (source, target) in enumerate(
            (
                (act_grad, act_grad_ref),
                (mean_table, mean_ref),
                (rstd_table, rstd_ref),
                (gamma_grad, gamma_grad_ref),
                (beta_grad, beta_grad_ref),
                (kernel_grad, kernel_grad_ref),
            )
        )
    ]
    stores[0].start()

    recv_affine()
    affine_rows = listed(affine)
    mean_table[...] = affine_rows[:, 2 * padded : 2 * padded + GROUPS]
    rstd_table[...] = affine_rows[:, 2 * padded + GROUPS : 2 * padded + 2 * GROUPS]
    stores[1].start()
    stores[2].start()
    totals = jnp.sum(affine_rows[:, : 2 * padded], axis=0, keepdims=True) * scale
    gamma_grad[...] = totals[:, :C].reshape(C)
    beta_grad[...] = totals[:, padded : padded + C].reshape(C)
    stores[3].start()
    stores[4].start()

    sent_stats()
    for which, step in enumerate(steps):
        ring_copy(zh, which, step).wait_send()
    sent_sums()
    for which, step in enumerate(steps):
        sums_copy(zh, which, step).wait_send()
    sent_affine()

    @pl.when(gives_next)
    def _():
        block_copy_next().wait_send()

    to_line(core, line_s, wait_send)
    passed(core, 0, wait_send)

    def mate_sent(row, carry):
        to_mate(core, row, 0).wait_send()
        return carry

    lax.fori_loop(0, Z, mate_sent, 0)

    @pl.when(takes_next)
    def _():
        to_line(2, next_line_s, wait_send)
        passed(2, 1, wait_send)

        def next_sent(row, carry):
            to_mate(2, row, 1).wait_send()
            return carry

        lax.fori_loop(0, Z, next_sent, 0)

    others(2 * Z, member, lambda p: act_copy(p, member).wait_send())
    others(YX, yx, lambda p: plane_copy(p, yx).wait_send())

    def take_part(slot, carry):
        @pl.when(jnp.logical_not(at_home & (slot == zh)))
        def _():
            column_copy(0, slot).wait_recv()

        return carry

    lax.fori_loop(0, Z, take_part, 0)
    result = jnp.sum(column_in[...], axis=0) * scale
    kernel_grad[...] = result[: KERNEL**3, :share]
    stores[5].start()

    def part_sent(part, carry):
        @pl.when(jnp.logical_not(at_home & (part == zl)))
        def _():
            column_copy(part, zh).wait_send()

        return carry

    lax.fori_loop(0, Z, part_sent, 0)
    for store in stores:
        store.wait()


def hand_over(*refs):
    count = len(refs) // 3
    sources, targets, holds = refs[:count], refs[count : 2 * count], refs[2 * count : 3 * count]
    load_sem, store_sem = refs[3 * count :]
    loads = [pltpu.make_async_copy(sources[n], holds[n], load_sem.at[n]) for n in range(count)]
    stores = [pltpu.make_async_copy(holds[n], targets[n], store_sem.at[n]) for n in range(count)]
    for load in loads:
        load.start()
    for load, store in zip(loads, stores):
        load.wait()
        store.start()
    for store in stores:
        store.wait()


def on_device(Z, YX, act, cotangent, kernel, gamma, beta):
    C, frames, rows, half = act.shape
    O = cotangent.shape[0]
    cells = frames * rows * half
    column = 2 * Z * Z
    group_count = C // GROUPS * cells * column
    scale = float(cells * column * YX) ** (-0.5)
    padded = -(-C // LANES) * LANES
    sizes = (Z, YX, C, O, group_count, scale)
    hbm = pl.BlockSpec(memory_space=pl.ANY)
    dma = pltpu.SemaphoreType.DMA
    width = 3 * YX
    outputs = (
        jax.ShapeDtypeStruct((C, frames, half), BF16),
        jax.ShapeDtypeStruct((KERNEL**3, 3 * O // Z), F32),
        jax.ShapeDtypeStruct((C,), F32),
        jax.ShapeDtypeStruct((C,), F32),
        jax.ShapeDtypeStruct((YX, GROUPS), F32),
        jax.ShapeDtypeStruct((YX, GROUPS), F32),
    )
    scratch = [
        pltpu.VMEM((C, frames, half), BF16),
        pltpu.VMEM((O, frames, half), BF16),
        pltpu.VMEM((C,), F32),
        pltpu.VMEM((C,), F32),
        *(pltpu.VMEM(out.shape, out.dtype) for out in outputs),
        pltpu.VMEM((C, cells), F32),
        pltpu.VMEM((2 * Z, 1, LANES), F32),
        pltpu.VMEM((Z, 1, LANES), F32),
        pltpu.VMEM((2 * Z, 1, 2 * padded + LANES), F32),
        pltpu.VMEM((Z, 1, 2 * padded + LANES), F32),
        pltpu.VMEM((YX, 1, 2 * padded + LANES), F32),
        pltpu.VMEM((3, Z, O, cells), BF16),
        pltpu.VMEM((5, Z + 2, KERNEL * LANES, cells), BF16),
        pltpu.VMEM((KERNEL**3, LANES, C), BF16),
        pltpu.VMEM((C, C), BF16),
        pltpu.VMEM((C, LANES), F32),
        pltpu.VMEM((C, LANES), F32),
        pltpu.VMEM((2, C, LANES), F32),
        pltpu.VMEM((width, LANES), F32),
        pltpu.VMEM((2, width, LANES), F32),
        pltpu.VMEM((C, cells), F32),
        pltpu.VMEM((C, cells), F32),
        pltpu.VMEM((C, cells), F32),
        pltpu.VMEM((2 * Z, width, cells), BF16),
        pltpu.VMEM((2 * Z, width, cells), BF16),
        pltpu.VMEM((KERNEL**2, width, KERNEL * LANES), F32),
        pltpu.VMEM((width, 32, LANES), F32),
        pltpu.VMEM((YX, 3, 32, LANES), BF16),
        pltpu.VMEM((YX, 3, 32, LANES), BF16),
        pltpu.VMEM((Z, 32, LANES), F32),
        pltpu.VMEM((Z, 32, LANES), F32),
        pltpu.SemaphoreType.REGULAR,
        pltpu.SemaphoreType.REGULAR,
        dma((5,)),
        dma((6,)),
        dma((2 * Z,)),
        dma((2 * Z,)),
        dma((Z,)),
        dma((Z,)),
        dma((2 * Z,)),
        dma((2 * Z,)),
        dma((Z,)),
        dma((Z,)),
        dma((YX,)),
        dma((YX,)),
        dma((Z,)),
        dma((2, Z)),
        dma((1,)),
        dma((Z,)),
        dma((2, Z)),
        dma((3, Z)),
        dma((2 * Z,)),
        dma((2 * Z,)),
        dma((YX,)),
        dma((YX,)),
        dma((Z,)),
        dma((Z,)),
    ]
    results = pl.pallas_call(
        functools.partial(body, sizes),
        out_shape=outputs,
        in_specs=[hbm] * 5,
        out_specs=(hbm,) * 6,
        scratch_shapes=scratch,
        compiler_params=pltpu.CompilerParams(
            collective_id=0, has_side_effects=True, vmem_limit_bytes=62 * 2**20
        ),
        name="unit_backward",
    )(
        act.reshape(C, frames, half),
        cotangent.reshape(O, frames, half),
        kernel,
        gamma,
        beta,
    )
    results = pl.pallas_call(
        hand_over,
        out_shape=outputs,
        in_specs=[hbm] * 6,
        out_specs=(hbm,) * 6,
        scratch_shapes=[*(pltpu.VMEM(out.shape, out.dtype) for out in outputs), dma((6,)), dma((6,))],
        name="hand_over",
    )(*results)
    return (results[0].reshape(act.shape), *results[1:])


def solution(mesh):
    Z = mesh.shape["rows"]
    YX = mesh.shape["frames"] // (2 * Z)
    in_specs = (P(None, "frames", "rows", None), P(None, "frames", "rows", None), P(), P(), P())
    out_specs = (P(None, "frames", "rows", None), P(None, ("frames", "rows")), P(), P(), P(), P())
    return jax.shard_map(
        functools.partial(on_device, Z, YX), mesh=mesh, in_specs=in_specs, out_specs=out_specs, check_vma=False
    )
```

```python
import functools

import jax
import jax.numpy as jnp
from jax import lax
from jax.experimental import pallas as pl
from jax.experimental.pallas import tpu as pltpu
from jax.sharding import PartitionSpec as P

GROUPS = 32
KERNEL = 3
LANES = 128
EPS = 1e-06
F32 = jnp.float32
BF16 = jnp.bfloat16
MESH = pl.DeviceIdType.MESH


def remote(src, dst, send_sem, recv_sem, device):
    return pltpu.make_async_remote_copy(
        src_ref=src,
        dst_ref=dst,
        send_sem=send_sem,
        recv_sem=recv_sem,
        device_id=device,
        device_id_type=MESH,
    )


def others(count, me, step, farthest=False):
    def body(d, carry):
        if farthest:
            d = count // 2 + (d // 2) * (1 - 2 * lax.rem(d, 2))
        step(lax.rem(me + d, count))
        return carry

    lax.fori_loop(1, count, body, 0)


def exchange(buf, send, recv, count, me, device):
    def copy(slot, peer):
        return remote(buf.at[slot], buf.at[slot], send.at[peer], recv.at[slot], device(peer))

    return (
        lambda: others(count, me, lambda p: copy(me, p).start(), True),
        lambda: others(count, me, lambda p: copy(p, p).wait_recv()),
        lambda: others(count, me, lambda p: copy(me, p).wait_send()),
    )


def listed(buf):
    return jnp.concatenate([buf[n] for n in range(buf.shape[0])], axis=0)


def body(
    sizes,
    act_ref,
    cot_ref,
    kernel_ref,
    gamma_ref,
    beta_ref,
    act_grad_ref,
    kernel_grad_ref,
    gamma_grad_ref,
    beta_grad_ref,
    mean_ref,
    rstd_ref,
    act_raw,
    cot_raw,
    gamma_raw,
    beta_raw,
    act_grad,
    kernel_grad,
    gamma_grad,
    beta_grad,
    mean_table,
    rstd_table,
    x_ref,
    stats,
    ring,
    sums,
    clip_sums,
    affine,
    blocks,
    slabs,
    weights,
    perm,
    mask_a,
    mask_b,
    gain,
    own_mask,
    own_gain,
    normed_ref,
    slope_ref,
    grad_ref,
    act_out,
    act_in,
    partial,
    by_owner,
    plane_out,
    plane_in,
    column_out,
    column_in,
    line_ready,
    far_ready,
    load_sem,
    store_sem,
    stats_s,
    stats_r,
    ring_s,
    ring_r,
    sums_s,
    sums_r,
    clip_sums_s,
    clip_sums_r,
    affine_s,
    affine_r,
    line_s,
    mate_s,
    next_s,
    next_line_s,
    pass_s,
    blocks_r,
    act_s,
    act_r,
    plane_s,
    plane_r,
    column_s,
    column_r,
):
    Z, YX, C, O, group_count, scale = sizes
    per_group = C // GROUPS
    half = act_raw.shape[2]
    cells = 2 * half
    width = 3 * YX
    padded = (affine.shape[2] - LANES) // 2
    f = lax.axis_index("frames")
    zl = lax.axis_index("rows")
    core = lax.rem(f, 2)
    zh = lax.rem(f // 2, Z)
    yx = f // (2 * Z)
    member = core * Z + zl

    def in_plane(p):
        return (p * (2 * Z) + lax.rem(f, 2 * Z), zl)

    def in_block(p):
        return (yx * (2 * Z) + zh * 2 + p // Z, lax.rem(p, Z))

    mate = (f + 1 - 2 * core, zl)

    def across_blocks(step):
        return (yx * (2 * Z) + lax.rem(zh + step + Z, Z) * 2 + core, zl)

    partner = (yx * (2 * Z) + lax.rem(zh + 2 * core - 1 + Z, Z) * 2 + 1 - core, zl)
    beside = (1,) if Z == 2 else (1, -1)
    steps = beside if Z == 2 else (1, -1, 2)

    barrier = pltpu.get_barrier_semaphore()

    def greet(device):
        pl.semaphore_signal(barrier, inc=1, device_id=device, device_id_type=MESH)

    for step in beside:
        greet(across_blocks(step))
    greet(partner)
    X = 4 if YX % 4 == 0 else YX
    x, y = lax.rem(yx, X), yx // X

    def along_x(p):
        return in_plane(y * X + p)

    others(X, x, lambda p: greet(along_x(p)), True)
    others(YX // X, y, lambda p: greet(in_plane(p * X + x)), True)
    others(2 * Z, member, lambda p: greet(in_block(p)))

    loads = [
        pltpu.make_async_copy(source, target, load_sem.at[n])
        for n, (source, target) in enumerate(
            (
                (act_ref, act_raw),
                (cot_ref, cot_raw),
                (gamma_ref, gamma_raw),
                (beta_ref, beta_raw),
                (kernel_ref, weights.at[:, pl.ds(0, O), :]),
            )
        )
    ]
    for load in loads:
        load.start()

    chan = lax.broadcasted_iota(jnp.int32, (C, LANES), 0)
    lane = lax.broadcasted_iota(jnp.int32, (C, LANES), 1)
    first_chan = lane * per_group
    mask_a[...] = jnp.where((chan >= first_chan) & (chan < first_chan + per_group), 1.0, 0.0).astype(F32)
    place = lax.broadcasted_iota(jnp.int32, (YX, C), 0) * (6 * Z)
    source = lax.broadcasted_iota(jnp.int32, (YX, C), 1)
    for p in range(2 * Z):
        for c in range(3):
            base = p * width + c * YX
            offset = (p % Z) * 6 + (p // Z) * 3 + c
            perm[base : base + YX, :] = jnp.where(source == place + offset, 1.0, 0.0).astype(BF16)

    loads[0].wait()
    x_a = act_raw[:, 0, :].astype(F32)
    x_b = act_raw[:, 1, :].astype(F32)
    x_ref[:, :half] = x_a
    x_ref[:, half:] = x_b
    mean = jnp.sum(x_a + x_b, axis=1, keepdims=True) / cells
    squares = jnp.sum((x_a - mean) * (x_a - mean) + (x_b - mean) * (x_b - mean), axis=1, keepdims=True)
    mean_row = jnp.sum(mask_a[...] * mean, axis=0, keepdims=True) / per_group
    gap = mean - jnp.sum(mask_a[...] * mean_row, axis=1, keepdims=True)
    squares = squares + cells * (gap * gap)
    stats[member] = mean_row + pltpu.roll(jnp.sum(mask_a[...] * squares, axis=0, keepdims=True), GROUPS, 1)

    loads[1].wait()
    for side in range(2):
        blocks[core, zl, :, side * half : (side + 1) * half] = cot_raw[:, side, :].astype(F32).astype(BF16)

    ordered = jnp.dot(perm[...], x_ref[...].astype(BF16), preferred_element_type=F32).astype(BF16)
    act_out[...] = ordered.reshape(act_out.shape)
    act_in[member] = act_out[member]

    pl.semaphore_wait(barrier, len(beside) + 1 + X - 1 + YX // X - 1 + 2 * Z - 1)

    if Z > 2:
        pl.semaphore_signal(far_ready, inc=1, device_id=across_blocks(-1), device_id_type=MESH)

    def block_copy(pair, row, send, device):
        ref = blocks.at[pair, row]
        return remote(ref, ref, send, blocks_r.at[pair, row], device)

    side_rows = Z // 2
    own_half = zl // side_rows
    gateway = side_rows - own_half
    is_gateway = zl == side_rows - 1 + own_half

    def half_peers(step):
        others(side_rows, lax.rem(zl, side_rows), lambda n: step(own_half * side_rows + n))

    def to_line(pair, sems, act):
        half_peers(lambda p: act(block_copy(pair, zl, sems.at[p], (f, p))))
        act(block_copy(pair, zl, sems.at[gateway], (f, gateway)))

    def to_mate(pair, row, which):
        return block_copy(pair, row, mate_s.at[which, row], mate)

    def landed(pair, row):
        block_copy(pair, row, line_s.at[0], mate).wait_recv()

    def start(copy):
        copy.start()

    def wait_send(copy):
        copy.wait_send()

    def passed(pair, which, act):
        @pl.when(is_gateway)
        def _():
            def across(n, carry):
                row = (1 - own_half) * side_rows + n
                half_peers(lambda p: act(block_copy(pair, row, pass_s.at[which, row], (f, p))))
                return carry

            lax.fori_loop(0, side_rows, across, 0)

    def take_line(pair, which):
        def across(n, carry):
            row = (1 - own_half) * side_rows + n
            landed(pair, row)

            @pl.when(is_gateway)
            def _():
                half_peers(lambda p: block_copy(pair, row, pass_s.at[which, row], (f, p)).start())

            to_mate(pair, row, which).start()
            return carry

        def near():
            def step(p):
                landed(pair, p)
                to_mate(pair, p, which).start()

            half_peers(step)

        def far():
            lax.fori_loop(0, side_rows, across, 0)

        near()
        far()

    gives_next = (core == 0) & (zh > 0)
    takes_next = (core == 1) & (zh < Z - 1)
    earlier = (lax.max(f - 1, 0), zl)

    def block_copy_next():
        return remote(blocks.at[core, zl], blocks.at[2, zl], next_s.at[0], blocks_r.at[2, zl], earlier)

    @pl.when(gives_next)
    def _():
        block_copy_next().start()

    start_stats, recv_stats, sent_stats = exchange(stats, stats_s, stats_r, 2 * Z, member, in_block)
    start_stats()
    to_line(core, line_s, start)
    to_mate(core, zl, 0).start()

    def act_copy(peer, slot):
        return remote(act_out.at[peer], act_in.at[slot], act_s.at[peer], act_r.at[slot], in_block(peer))


    others(X, x, lambda p: pl.semaphore_signal(line_ready, inc=1, device_id=along_x(p), device_id_type=MESH))

    first_chan = (lane - GROUPS) * per_group
    mask_b[...] = jnp.where((chan >= first_chan) & (chan < first_chan + per_group), 1.0, 0.0).astype(F32)
    loads[2].wait()
    loads[3].wait()
    gamma_row = gamma_raw[...].reshape(1, C)
    beta_row = beta_raw[...].reshape(1, C)
    gain[0] = jnp.broadcast_to(gamma_row, (LANES, C)).T
    gain[1] = jnp.broadcast_to(beta_row, (LANES, C)).T
    own_chan = lax.broadcasted_iota(jnp.int32, (YX, LANES), 0) * (6 * Z)
    own_lane = lax.broadcasted_iota(jnp.int32, (YX, LANES), 1) * per_group
    for c in range(3):
        at = pl.ds(c * YX, YX)
        offset = zl * 6 + core * 3 + c
        chosen = jnp.where(source == place + offset, 1.0, 0.0).astype(F32)
        own_gain[0, at, :] = jnp.broadcast_to(jnp.sum(chosen * gamma_row, axis=1, keepdims=True), (YX, LANES))
        own_gain[1, at, :] = jnp.broadcast_to(jnp.sum(chosen * beta_row, axis=1, keepdims=True), (YX, LANES))
        inside = (own_chan + offset >= own_lane) & (own_chan + offset < own_lane + per_group)
        own_mask[at, :] = jnp.where(inside, 1.0, 0.0).astype(F32)

    if O < LANES:
        weights[:, O:, :] = jnp.zeros((KERNEL**3, LANES - O, C), BF16)

    @pl.when(zh == Z - 1)
    def _():
        blocks[2] = jnp.zeros(blocks.shape[1:], BF16)

    slabs[:, 0] = jnp.zeros((5,) + slabs.shape[2:], BF16)
    slabs[:, Z + 1] = jnp.zeros((5,) + slabs.shape[2:], BF16)
    if O < LANES:
        for k in range(KERNEL):
            slabs[:, 1 : Z + 1, k * LANES + O : (k + 1) * LANES, :] = jnp.zeros((5, Z, LANES - O, cells), BF16)

    partial[...] = jnp.zeros(partial.shape, F32)
    by_owner[...] = jnp.zeros(by_owner.shape, F32)

    lane_row = lax.broadcasted_iota(jnp.int32, (1, LANES), 1)

    def combined(rows, cells_of_one):
        total = jnp.sum(rows, axis=0, keepdims=True)
        mean_row = jnp.where(lane_row < GROUPS, total / rows.shape[0], 0.0)
        gaps = jnp.where(lane_row < GROUPS, rows - mean_row, 0.0)
        return mean_row, pltpu.roll(total, LANES - GROUPS, 1) + cells_of_one * jnp.sum(gaps * gaps, axis=0, keepdims=True)

    recv_stats()
    block_mean, block_squares = combined(listed(stats), per_group * cells)
    ring[zh] = block_mean + pltpu.roll(jnp.where(lane_row < GROUPS, block_squares, 0.0), GROUPS, 1)

    def ring_copy(slot, which, step):
        return remote(ring.at[slot], ring.at[slot], ring_s.at[which], ring_r.at[slot], across_blocks(step))

    def block_at(step):
        return lax.rem(zh + step + Z, Z)

    for which, step in enumerate(steps):
        if step == 2:
            pl.semaphore_wait(far_ready, 1)
        ring_copy(zh, which, step).start()

    @pl.when(takes_next)
    def _():
        landed(2, zl)
        to_line(2, next_line_s, start)
        to_mate(2, zl, 1).start()

    others(2 * Z, member, lambda p: act_copy(p, member).start())

    take_line(core, 0)

    def from_mate(row, carry):
        landed(1 - core, row)
        return carry

    lax.fori_loop(0, Z, from_mate, 0)

    column_lane = lax.broadcasted_iota(jnp.int32, (O, half), 1)

    def fill(frames):
        def fill_row(row, carry):
            for frame in frames:
                slab = blocks[frame // 2, row, :, (frame % 2) * half : (frame % 2 + 1) * half]
                wide = slab.astype(F32)
                shifted = (
                    jnp.where(column_lane < half - 1, pltpu.roll(wide, half - 1, 1), 0.0).astype(BF16),
                    slab,
                    jnp.where(column_lane > 0, pltpu.roll(wide, 1, 1), 0.0).astype(BF16),
                )
                for k in range(KERNEL):
                    if frame < 5:
                        slabs[frame, row + 1, k * LANES : k * LANES + O, :half] = shifted[k]
                    if frame > 0:
                        slabs[frame - 1, row + 1, k * LANES : k * LANES + O, half:] = shifted[k]
            return carry

        lax.fori_loop(0, Z, fill_row, 0)

    fill(range(4))

    def gradient(lags):
        total = grad_ref[...]
        for i in lags:
            for j in range(KERNEL):
                tap = (i * KERNEL + j) * KERNEL
                total += lax.dot_general(
                    weights[tap : tap + KERNEL].reshape(KERNEL * LANES, C),
                    slabs[2 * core + 2 - i, zl - j + 2],
                    (((0,), (0,)), ((), ())),
                    preferred_element_type=F32,
                )
        grad_ref[...] = total

    loads[4].wait()
    grad_ref[...] = jnp.zeros((C, cells), F32)
    gradient((2,))


    @pl.when(takes_next)
    def _():
        take_line(2, 1)

    @pl.when(core == 1)
    def _():
        fill(range(4, 6))

    gradient((0, 1))

    for step in steps:
        ring_copy(block_at(step), 0, step).wait_recv()
    mean_row, squares_row = combined(listed(ring), 2 * Z * per_group * cells)
    rstd_row = jnp.where(
        lane_row < GROUPS, lax.rsqrt(jnp.where(lane_row < GROUPS, squares_row, 0.0) / group_count + EPS), 0.0
    )
    affine[yx, :, 2 * padded :] = jnp.where(
        lane_row < GROUPS, mean_row, jnp.where(lane_row < 2 * GROUPS, pltpu.roll(rstd_row, GROUPS, 1), 0.0)
    )

    others(2 * Z, member, lambda p: act_copy(member, p).wait_recv())

    own_mean = jnp.sum(own_mask[...] * mean_row, axis=1, keepdims=True)
    own_rstd = jnp.sum(own_mask[...] * rstd_row, axis=1, keepdims=True)
    own_gamma, own_beta = own_gain[0, :, :1], own_gain[1, :, :1]
    for slot in range(2 * Z):
        shaped = (act_in[slot].astype(F32) - own_mean) * own_rstd * own_gamma + own_beta
        act_in[slot] = (shaped / (1.0 + jnp.exp(-shaped))).astype(BF16)


    def correlate(lead):
        for row in range(Z):
            low, high = max(0, row - 1), min(Z - 1, row + 1)
            count = high - low + 1
            for side in range(2):
                i = 2 * side + 2 - lead
                if not 0 <= i < KERNEL:
                    continue
                product = lax.dot_general(
                    act_in[side * Z + low : side * Z + high + 1].reshape(count * width, cells),
                    slabs[lead, row + 1],
                    (((1,), (1,)), ((), ())),
                    preferred_element_type=F32,
                )
                for n in range(count):
                    j = low + n + 1 - row
                    partial[i * KERNEL + j] += product[n * width : (n + 1) * width]

    for lead in range(3):
        correlate(lead)

    mean = jnp.sum(mask_a[...] * mean_row, axis=1, keepdims=True)
    rstd = jnp.sum(mask_a[...] * rstd_row, axis=1, keepdims=True)
    for side in range(2):
        at = pl.ds(side * half, half)
        normed = (x_ref[:, at] - mean) * rstd
        shaped = normed * gain[0] + gain[1]
        sig = 1.0 / (1.0 + jnp.exp(-shaped))
        normed_ref[:, at] = normed
        slope_ref[:, at] = sig * (1.0 + shaped * (1.0 - sig))

    shaped_grad = grad_ref[...] * slope_ref[...]
    slope_ref[...] = shaped_grad
    scaled = shaped_grad * normed_ref[...]
    beta_sum = jnp.sum(shaped_grad[:, :half] + shaped_grad[:, half:], axis=1, keepdims=True)
    gamma_sum = jnp.sum(scaled[:, :half] + scaled[:, half:], axis=1, keepdims=True)
    sums[member, :, 0:C] = jnp.broadcast_to(gamma_sum, (C, LANES)).T[:1]
    sums[member, :, padded : padded + C] = jnp.broadcast_to(beta_sum, (C, LANES)).T[:1]
    sums[member, :, 2 * padded :] = jnp.sum(
        gain[0] * (mask_a[...] * beta_sum + mask_b[...] * gamma_sum), axis=0, keepdims=True
    )
    start_sums, recv_sums, sent_sums = exchange(sums, sums_s, sums_r, 2 * Z, member, in_block)
    start_sums()

    tile_rows = min(8, YX)
    tiles = YX // tile_rows

    def arrange(lags):
        lax.fori_loop(0, 3 * tiles, functools.partial(arrange_tile, lags), 0)

    def arrange_tile(lags, tile, carry):
        c = tile // tiles
        first_place = lax.rem(tile, tiles) * tile_rows
        at = pl.ds(pl.multiple_of(tile * tile_rows, tile_rows), tile_rows)
        for ij in [i * KERNEL + j for i in lags for j in range(KERNEL)]:
            for k in range(KERNEL):
                tap = ij * KERNEL + k
                values = partial[ij, at, k * LANES : (k + 1) * LANES]
                for row in range(tile_rows):
                    by_owner[(first_place + row) * 3 + c, tap : tap + 1, :] = values[row : row + 1]
        return carry

    arrange((2,))

    @pl.when((core == 0) & (zh < Z - 1))
    def _():
        def next_from_mate(row, carry):
            landed(2, row)
            return carry

        lax.fori_loop(0, Z, next_from_mate, 0)

    @pl.when(core == 0)
    def _():
        fill(range(4, 6))

    for lead in range(3, 5):
        correlate(lead)


    arrange((0, 1))
    plane_out[...] = by_owner[...].astype(BF16).reshape(plane_out.shape)

    def plane_copy(peer, slot):
        return remote(plane_out.at[peer], plane_in.at[slot], plane_s.at[peer], plane_r.at[slot], in_plane(peer))

    pl.semaphore_wait(line_ready, X - 1)
    others(YX, yx, lambda p: plane_copy(p, yx).start())
    plane_in[yx] = jnp.zeros(plane_in.shape[1:], BF16)

    recv_sums()
    clip_sums[zh] = jnp.sum(listed(sums), axis=0, keepdims=True)

    def sums_copy(slot, which, step):
        return remote(
            clip_sums.at[slot], clip_sums.at[slot], clip_sums_s.at[which], clip_sums_r.at[slot], across_blocks(step)
        )

    for which, step in enumerate(steps):
        sums_copy(zh, which, step).start()

    others(YX, yx, lambda p: plane_copy(yx, p).wait_recv())

    def add(slot, carry):
        return carry + plane_in[slot].astype(F32)

    summed = lax.fori_loop(0, YX, add, by_owner[pl.ds(3 * yx, 3)])
    share = 3 * O // Z
    tap_lane = lax.broadcasted_iota(jnp.int32, summed.shape[1:], 1)
    for part in range(Z):
        packed = jnp.zeros(summed.shape[1:], F32)
        for c in range(3):
            low, high = max(share * part, O * c), min(share * (part + 1), O * (c + 1))
            if high <= low:
                continue
            inside = (tap_lane >= low - share * part) & (tap_lane < high - share * part)
            shift = (O * c - share * part) % LANES
            moved = pltpu.roll(summed[c], shift, 1) if shift else summed[c]
            packed = jnp.where(inside, moved, packed)
        column_out[part] = packed

    def column_copy(part, slot):
        device = (yx * (2 * Z) + zl * 2 + core, part)
        return remote(column_out.at[part], column_in.at[slot], column_s.at[part], column_r.at[slot], device)

    at_home = zh == zl

    def send_part(part, carry):
        stays = at_home & (part == zl)

        @pl.when(jnp.logical_not(stays))
        def _():
            column_copy(part, zh).start()

        @pl.when(stays)
        def _():
            column_in[zh] = column_out[part]

        return carry

    for step in range(1, Z + 1):
        send_part(lax.rem(zl + step, Z), 0)

    for step in steps:
        sums_copy(block_at(step), 0, step).wait_recv()
    clip_total = jnp.sum(listed(clip_sums), axis=0, keepdims=True)
    affine[yx, :, : 2 * padded] = clip_total[:, : 2 * padded]
    start_affine, recv_affine, sent_affine = exchange(affine, affine_s, affine_r, YX, yx, in_plane)
    start_affine()

    group_row = clip_total[:, 2 * padded :] / group_count
    first = jnp.sum(mask_a[...] * group_row, axis=1, keepdims=True)
    second = jnp.sum(mask_b[...] * group_row, axis=1, keepdims=True)
    for side in range(2):
        at = pl.ds(side * half, half)
        act_grad[:, side, :] = (
            rstd * (gain[0] * slope_ref[:, at] - first - normed_ref[:, at] * second)
        ).astype(BF16)

    stores = [
        pltpu.make_async_copy(source, target, store_sem.at[n])
        for n, (source, target) in enumerate(
            (
                (act_grad, act_grad_ref),
                (mean_table, mean_ref),
                (rstd_table, rstd_ref),
                (gamma_grad, gamma_grad_ref),
                (beta_grad, beta_grad_ref),
                (kernel_grad, kernel_grad_ref),
            )
        )
    ]
    stores[0].start()

    recv_affine()
    affine_rows = listed(affine)
    mean_table[...] = affine_rows[:, 2 * padded : 2 * padded + GROUPS]
    rstd_table[...] = affine_rows[:, 2 * padded + GROUPS : 2 * padded + 2 * GROUPS]
    stores[1].start()
    stores[2].start()
    totals = jnp.sum(affine_rows[:, : 2 * padded], axis=0, keepdims=True) * scale
    gamma_grad[...] = totals[:, :C].reshape(C)
    beta_grad[...] = totals[:, padded : padded + C].reshape(C)
    stores[3].start()
    stores[4].start()

    sent_stats()
    for which, step in enumerate(steps):
        ring_copy(zh, which, step).wait_send()
    sent_sums()
    for which, step in enumerate(steps):
        sums_copy(zh, which, step).wait_send()
    sent_affine()

    @pl.when(gives_next)
    def _():
        block_copy_next().wait_send()

    to_line(core, line_s, wait_send)
    passed(core, 0, wait_send)

    def mate_sent(row, carry):
        to_mate(core, row, 0).wait_send()
        return carry

    lax.fori_loop(0, Z, mate_sent, 0)

    @pl.when(takes_next)
    def _():
        to_line(2, next_line_s, wait_send)
        passed(2, 1, wait_send)

        def next_sent(row, carry):
            to_mate(2, row, 1).wait_send()
            return carry

        lax.fori_loop(0, Z, next_sent, 0)

    others(2 * Z, member, lambda p: act_copy(p, member).wait_send())
    others(YX, yx, lambda p: plane_copy(p, yx).wait_send())

    def take_part(slot, carry):
        @pl.when(jnp.logical_not(at_home & (slot == zh)))
        def _():
            column_copy(0, slot).wait_recv()

        return carry

    lax.fori_loop(0, Z, take_part, 0)
    result = jnp.sum(column_in[...], axis=0) * scale
    kernel_grad[...] = result[: KERNEL**3, :share]
    stores[5].start()

    def part_sent(part, carry):
        @pl.when(jnp.logical_not(at_home & (part == zl)))
        def _():
            column_copy(part, zh).wait_send()

        return carry

    lax.fori_loop(0, Z, part_sent, 0)
    for store in stores:
        store.wait()


def hand_over(*refs):
    count = len(refs) // 3
    sources, targets, holds = refs[:count], refs[count : 2 * count], refs[2 * count : 3 * count]
    load_sem, store_sem = refs[3 * count :]
    loads = [pltpu.make_async_copy(sources[n], holds[n], load_sem.at[n]) for n in range(count)]
    stores = [pltpu.make_async_copy(holds[n], targets[n], store_sem.at[n]) for n in range(count)]
    for load in loads:
        load.start()
    for load, store in zip(loads, stores):
        load.wait()
        store.start()
    for store in stores:
        store.wait()


def on_device(Z, YX, act, cotangent, kernel, gamma, beta):
    C, frames, rows, half = act.shape
    O = cotangent.shape[0]
    cells = frames * rows * half
    column = 2 * Z * Z
    group_count = C // GROUPS * cells * column
    scale = float(cells * column * YX) ** (-0.5)
    padded = -(-C // LANES) * LANES
    sizes = (Z, YX, C, O, group_count, scale)
    hbm = pl.BlockSpec(memory_space=pl.ANY)
    dma = pltpu.SemaphoreType.DMA
    width = 3 * YX
    outputs = (
        jax.ShapeDtypeStruct((C, frames, half), BF16),
        jax.ShapeDtypeStruct((KERNEL**3, 3 * O // Z), F32),
        jax.ShapeDtypeStruct((C,), F32),
        jax.ShapeDtypeStruct((C,), F32),
        jax.ShapeDtypeStruct((YX, GROUPS), F32),
        jax.ShapeDtypeStruct((YX, GROUPS), F32),
    )
    scratch = [
        pltpu.VMEM((C, frames, half), BF16),
        pltpu.VMEM((O, frames, half), BF16),
        pltpu.VMEM((C,), F32),
        pltpu.VMEM((C,), F32),
        *(pltpu.VMEM(out.shape, out.dtype) for out in outputs),
        pltpu.VMEM((C, cells), F32),
        pltpu.VMEM((2 * Z, 1, LANES), F32),
        pltpu.VMEM((Z, 1, LANES), F32),
        pltpu.VMEM((2 * Z, 1, 2 * padded + LANES), F32),
        pltpu.VMEM((Z, 1, 2 * padded + LANES), F32),
        pltpu.VMEM((YX, 1, 2 * padded + LANES), F32),
        pltpu.VMEM((3, Z, O, cells), BF16),
        pltpu.VMEM((5, Z + 2, KERNEL * LANES, cells), BF16),
        pltpu.VMEM((KERNEL**3, LANES, C), BF16),
        pltpu.VMEM((C, C), BF16),
        pltpu.VMEM((C, LANES), F32),
        pltpu.VMEM((C, LANES), F32),
        pltpu.VMEM((2, C, LANES), F32),
        pltpu.VMEM((width, LANES), F32),
        pltpu.VMEM((2, width, LANES), F32),
        pltpu.VMEM((C, cells), F32),
        pltpu.VMEM((C, cells), F32),
        pltpu.VMEM((C, cells), F32),
        pltpu.VMEM((2 * Z, width, cells), BF16),
        pltpu.VMEM((2 * Z, width, cells), BF16),
        pltpu.VMEM((KERNEL**2, width, KERNEL * LANES), F32),
        pltpu.VMEM((width, 32, LANES), F32),
        pltpu.VMEM((YX, 3, 32, LANES), BF16),
        pltpu.VMEM((YX, 3, 32, LANES), BF16),
        pltpu.VMEM((Z, 32, LANES), F32),
        pltpu.VMEM((Z, 32, LANES), F32),
        pltpu.SemaphoreType.REGULAR,
        pltpu.SemaphoreType.REGULAR,
        dma((5,)),
        dma((6,)),
        dma((2 * Z,)),
        dma((2 * Z,)),
        dma((Z,)),
        dma((Z,)),
        dma((2 * Z,)),
        dma((2 * Z,)),
        dma((Z,)),
        dma((Z,)),
        dma((YX,)),
        dma((YX,)),
        dma((Z,)),
        dma((2, Z)),
        dma((1,)),
        dma((Z,)),
        dma((2, Z)),
        dma((3, Z)),
        dma((2 * Z,)),
        dma((2 * Z,)),
        dma((YX,)),
        dma((YX,)),
        dma((Z,)),
        dma((Z,)),
    ]
    results = pl.pallas_call(
        functools.partial(body, sizes),
        out_shape=outputs,
        in_specs=[hbm] * 5,
        out_specs=(hbm,) * 6,
        scratch_shapes=scratch,
        compiler_params=pltpu.CompilerParams(
            collective_id=0, has_side_effects=True, vmem_limit_bytes=62 * 2**20
        ),
        name="unit_backward",
    )(
        act.reshape(C, frames, half),
        cotangent.reshape(O, frames, half),
        kernel,
        gamma,
        beta,
    )
    results = pl.pallas_call(
        hand_over,
        out_shape=outputs,
        in_specs=[hbm] * 6,
        out_specs=(hbm,) * 6,
        scratch_shapes=[*(pltpu.VMEM(out.shape, out.dtype) for out in outputs), dma((6,)), dma((6,))],
        name="hand_over",
    )(*results)
    return (results[0].reshape(act.shape), *results[1:])


def solution(mesh):
    Z = mesh.shape["rows"]
    YX = mesh.shape["frames"] // (2 * Z)
    in_specs = (P(None, "frames", "rows", None), P(None, "frames", "rows", None), P(), P(), P())
    out_specs = (P(None, "frames", "rows", None), P(None, ("frames", "rows")), P(), P(), P(), P())
    return jax.shard_map(
        functools.partial(on_device, Z, YX), mesh=mesh, in_specs=in_specs, out_specs=out_specs, check_vma=False
    )
```
